256 devices in a mesh: ctx: 8 (over x, y_lo), exp: 32 (over z, y_hi, core).
Axes of the slice: x: 4, y: 4 (y_hi: 2, y_lo: 2; y = y_hi * 2 + y_lo), z: 8, core: 2. Of those that a mesh axis runs over, the one named last changes fastest.
Arguments:
- query: bfloat16 [4096, 12288], P('exp', 'ctx')
- latent_cache: bfloat16 [32, 4096, 576], P('exp', 'ctx')
- absorb_key: bfloat16 [64, 128, 512], P('ctx', None, 'exp'), may hold values from -0.5 to 0.5
- absorb_value: bfloat16 [64, 512, 128], P('ctx', 'exp'), may hold values from -0.25 to 0.25
- out_weight: bfloat16 [8192, 3584], P('ctx', 'exp'), may hold values from -0.0625 to 0.0625
- hidden: bfloat16 [4096, 3584], P('exp', 'ctx'), may hold values from -3 to 3
- norm_gain: float32 [3584], replicated, may hold values from 0.1 to 1.9
- block_mask: int32 [32, 32], replicated, may hold values from 0 to 1, as said below
- routes: int32 [4096, 2], P('exp'), may hold values from 0 to 127, all different within a row; in each aligned block of 128 rows (0 to 127, 128 to 255, ...) at most 3 rows name the same one
- route_weight: float32 [4096, 2], P('exp'), may hold values from 0.2 to 1
- w_gate: bfloat16 [128, 3584, 1024], P('exp', None, 'ctx'), may hold values from -0.09375 to 0.09375
- w_up: bfloat16 [128, 3584, 1024], P('exp', None, 'ctx'), may hold values from -0.09375 to 0.09375
- w_down: bfloat16 [128, 1024, 3584], P('exp', 'ctx'), may hold values from -0.1875 to 0.1875
Outputs:
- result: bfloat16 [4096, 3584], P('exp', 'ctx')
The draws below stay inside these ranges and needn't reach their ends.
Inputs may be any that keep to these rules, and one draw needn't show every extreme that they name: block_mask[i][j] is 0 for j > i and 1 for j = i. `routes`: each row names 2 different experts; the rows of one sequence name no expert more than 3 times, a bound that some block reaches.
All inputs are finite; a program needn't handle non-finite values.
Results may differ from the reference program's by a relative error of at most 0.013.
Values may be sent and summed in bfloat16 or wider, within the bound.
A program may use at most 128 MiB of HBM per device.

```python
import math
import jax
import jax.numpy as jnp
import numpy as np
from jax import lax

D = 3584
HEADS = 64
DN = 128
DR = 64
DC = 512
DV = 128
FF = 1024
TOPK = 2
BLK = 128
Q_DEV = 128
LEN = 4096
SEQS = 32
TOKENS = 4096
NB = 32
EXPERTS = 128
CAP = 3
N_EXP = 32


def shared_rope(key):
    return jax.random.normal(jax.random.fold_in(key, 11), (SEQS, LEN, DR), jnp.float32)


def draw_latent_cache(key, part):
    rope_part = shared_rope(key)
    key = jax.random.fold_in(key, 1)
    latent = jax.random.normal(key, (SEQS, LEN, DC), jnp.float32)
    return jnp.concatenate([latent, rope_part], axis=2).astype(jnp.bfloat16)


def draw_query(key, part):
    key = jax.random.fold_in(key, 2)
    baseline = jax.random.normal(key, (TOKENS, HEADS, DN + DR), jnp.float32)
    return baseline.reshape(TOKENS, HEADS * (DN + DR)).astype(jnp.bfloat16)


def draw_block_mask(key, part):
    key = jax.random.fold_in(key, 5)
    coin_flips = jax.random.randint(key, (NB, NB), 0, 2)
    row_ids = jnp.arange(NB)[:, None]
    col_ids = jnp.arange(NB)[None, :]
    return jnp.where(col_ids > row_ids, 0, jnp.where(col_ids == row_ids, 1, coin_flips)).astype(jnp.int32)


def block_scale(stream_key, dims, pieces, least, top_value):
    factor_of, own = 1.0, jax.random.fold_in(stream_key, 6)
    for axis_at, parts in pieces:
        draws = jnp.exp(jax.random.uniform(jax.random.fold_in(own, axis_at), (parts,), jnp.float32, least / len(pieces), top_value / len(pieces)))
        factor_of = factor_of * jnp.repeat(draws, dims[axis_at] // parts).reshape([-1 if axis == axis_at else 1 for axis in range(len(dims))])
    return factor_of


def deal_out(key, own, number, rows, amount, top, bound, slope):
    order = jax.random.permutation(key, amount)
    heavy_load, usual = shares(amount, rows * top, bound, slope, True), shares(amount, rows * top, bound, slope, False)
    places = jnp.arange(amount)

    def named(lengths, turn):
        used = int((lengths > 0).sum())
        fixed = max(1, used // 4)
        passed = fixed + (places - fixed + turn * (used - fixed)) % max(1, amount - fixed)
        return jnp.zeros((amount,), jnp.int32).at[order[jnp.where(places < fixed, places, passed)]].set(jnp.asarray(lengths, jnp.int32))

    lengths = jnp.where(number % 4 == 0, named(heavy_load, number // 4), named(usual, number - number // 4 - 1))
    mixed = jax.random.permutation(jax.random.fold_in(own, 3), amount)
    giver, receiver = mixed[0:amount // 2 * 2:2], mixed[1:amount // 2 * 2:2]
    margin = jnp.minimum(lengths[giver] - 1, bound - lengths[receiver]) // 2
    margin = jnp.where((giver == order[0]) | (receiver == order[0]) | (lengths[receiver] == 0), 0, jnp.maximum(margin, 0))
    passed = jax.random.randint(jax.random.fold_in(own, 4), (amount // 2,), 0, 1 << 20) % (margin + 1)
    lengths = lengths.at[giver].add(-passed).at[receiver].add(passed)
    labels = jnp.searchsorted(jnp.cumsum(lengths), jnp.arange(rows * top), side="right").astype(jnp.int32)
    grid = labels.reshape(top, rows).T
    grid = grid[jax.random.permutation(jax.random.fold_in(own, 1), rows)]
    turn = jax.random.randint(jax.random.fold_in(own, 2), (rows, 1), 0, top)
    return jnp.take_along_axis(grid, (jnp.arange(top)[None, :] + turn) % top, axis=1)


def shares(amount, total, most, slope, full):
    portions = [(1 << 20) // math.isqrt(standing ** slope) + 1 for standing in range(1, amount + 1)]
    largest = most if full else min(most, max(-(-total // amount), total * portions[0] // sum(portions)))
    least = 1 if total - largest >= amount - 1 else 0
    counts, rest = [largest] + [least] * (amount - 1), total - largest - least * (amount - 1)
    while rest > 0:
        movable = [i for i in range(1, amount) if counts[i] < largest] or [i for i in range(1, amount) if counts[i] < most]
        whole, budget = sum([portions[i] for i in movable]), rest
        for i in movable:
            extra = min(most - counts[i], max(1, budget * portions[i] // whole), rest)
            counts[i] = counts[i] + extra
            rest = rest - extra
    return np.array(counts)


def normal_values(key, shape, deviation, limit, cuts=(), kind=jnp.bfloat16):
    drawn = jax.random.normal(key, shape, jnp.float32) * deviation
    if len(cuts) > 0:
        drawn = block_scale(key, shape, cuts, -0.22, 0.18) * drawn
    return jnp.clip(drawn, min=-limit, max=limit).astype(kind)


def setup_inputs(seed: int = 0) -> dict:
    seeds = jax.random.split(jax.random.key(seed), 14)
    query = draw_query(jax.random.fold_in(seeds[13], 71), 0)
    latent_cache = draw_latent_cache(jax.random.fold_in(seeds[13], 71), 0)
    absorb_key = normal_values(seeds[2], (HEADS, DN, DC), DN ** -0.5, 0.5, ((0, 8), (2, 32)))
    absorb_value = normal_values(seeds[3], (HEADS, DC, DV), DC ** -0.5, 0.25, ((0, 8), (1, 32)))
    out_weight = normal_values(seeds[4], (HEADS * DV, D), (HEADS * DV) ** -0.5, 0.0625, ((0, 8), (1, 32)))
    hidden = normal_values(seeds[5], (TOKENS, D), 0.5, 3.0, ((0, 32), (1, 8)))
    norm_gain = jnp.clip(1.0 + 0.18 * jax.random.normal(seeds[6], (D,), jnp.float32), 0.1, 1.9)
    block_mask = draw_block_mask(jax.random.fold_in(seeds[13], 71), 0)
    routes_keys = jax.random.split(jax.random.fold_in(seeds[8], 1), TOKENS // Q_DEV)
    routes_turns = jax.random.permutation(jax.random.fold_in(seeds[8], 3), TOKENS // Q_DEV)
    routes = jax.vmap(lambda own, number: deal_out(jax.random.fold_in(seeds[8], 2), own, number, Q_DEV, EXPERTS, TOPK, CAP, 2))(routes_keys, routes_turns).reshape((TOKENS, TOPK))
    route_weight = jnp.clip(0.2 + 0.8 * jax.random.uniform(seeds[9], (TOKENS, TOPK), jnp.float32) ** block_scale(seeds[9], (TOKENS, TOPK), ((0, 32),), -0.2, 0.2), 0.2, 1.0)
    w_gate = normal_values(seeds[10], (EXPERTS, D, FF), D ** -0.5, 0.09375, ((0, 32), (2, 8)))
    w_up = normal_values(seeds[11], (EXPERTS, D, FF), D ** -0.5, 0.09375, ((0, 32), (2, 8)))
    w_down = normal_values(seeds[12], (EXPERTS, FF, D), FF ** -0.5, 0.1875, ((0, 32), (1, 8)))
    return dict(query=query, latent_cache=latent_cache, absorb_key=absorb_key, absorb_value=absorb_value, out_weight=out_weight, hidden=hidden, norm_gain=norm_gain, block_mask=block_mask, routes=routes, route_weight=route_weight, w_gate=w_gate, w_up=w_up, w_down=w_down)


def expert_ffn(inputs, gate_matrix, up_matrix, down_matrix):
    gate_value = jnp.dot(inputs, gate_matrix, preferred_element_type=jnp.float32)
    up_value = jnp.dot(inputs, up_matrix, preferred_element_type=jnp.float32)
    activated = (jax.nn.silu(gate_value) * up_value).astype(jnp.bfloat16)
    return jnp.dot(activated, down_matrix, preferred_element_type=jnp.float32)

def reference(query, latent_cache, absorb_key, absorb_value, out_weight, hidden, norm_gain, block_mask, routes, route_weight, w_gate, w_up, w_down):
    score_scale = 1.0 / math.sqrt(DN + DR)
    queries = query.reshape(TOKENS, HEADS, DN + DR)
    query_lat = jnp.einsum('shn,hnc->shc', queries[:, :, :DN].astype(jnp.float32), absorb_key.astype(jnp.float32)).astype(jnp.bfloat16)
    query_lat = lax.optimization_barrier(query_lat)
    query_rope = queries[:, :, DN:]
    positions = jnp.arange(LEN, dtype=jnp.int32)
    key_blocks = positions // BLK
    blocks_per_seq = Q_DEV // BLK
    first_block = (LEN - Q_DEV) // BLK

    def one_block(block_index):
        seq_id = block_index // blocks_per_seq
        local_block = block_index % blocks_per_seq
        offset = block_index * BLK
        cache_rows = lax.dynamic_index_in_dim(latent_cache, seq_id, 0, keepdims=False)
        latent = cache_rows[:, :DC].astype(jnp.float32)
        key_rope = cache_rows[:, DC:].astype(jnp.float32)
        lat_rows = lax.dynamic_slice_in_dim(query_lat, offset, BLK, 0).astype(jnp.float32)
        rope_rows = lax.dynamic_slice_in_dim(query_rope, offset, BLK, 0).astype(jnp.float32)
        scores = (jnp.einsum('bhc,sc->bhs', lat_rows, latent) + jnp.einsum('bhr,sr->bhs', rope_rows, key_rope)) * score_scale
        query_pos = LEN - Q_DEV + local_block * BLK + jnp.arange(BLK, dtype=jnp.int32)
        mask_line = lax.dynamic_index_in_dim(block_mask, first_block + local_block, 0, keepdims=False)
        mask_row = jnp.take(mask_line, key_blocks)
        allowed = (mask_row[None, :] == 1) & (positions[None, :] <= query_pos[:, None])
        scores = jnp.where(allowed[:, None, :], scores, -1e+30)
        row_max = lax.optimization_barrier(jnp.max(scores, axis=-1, keepdims=True))
        exps = jnp.where(allowed[:, None, :], jnp.exp(scores - row_max), 0.0)
        denominator = lax.optimization_barrier(jnp.sum(exps, axis=-1, keepdims=True))
        weights = lax.optimization_barrier(exps.astype(jnp.bfloat16)).astype(jnp.float32)
        latent_out = (jnp.einsum('bhs,sc->bhc', weights, latent) / denominator).astype(jnp.bfloat16)
        latent_out = lax.optimization_barrier(latent_out).astype(jnp.float32)
        values = jnp.einsum('bhc,hcv->bhv', latent_out, absorb_value.astype(jnp.float32))
        return values.astype(jnp.bfloat16).reshape(BLK, HEADS * DV)
    attended = lax.map(one_block, jnp.arange(TOKENS // BLK, dtype=jnp.int32)).reshape(TOKENS, HEADS * DV)
    projected = jnp.dot(attended, out_weight, preferred_element_type=jnp.float32)
    residual = hidden.astype(jnp.float32) + projected
    mean_square = lax.optimization_barrier(jnp.mean(residual * residual, axis=1, keepdims=True))
    normed = (residual * lax.rsqrt(mean_square + 1e-06) * norm_gain).astype(jnp.bfloat16)
    flat_routes = routes.reshape(-1)
    row_total = TOKENS * TOPK
    one_hot = (flat_routes[:, None] == jnp.arange(EXPERTS, dtype=jnp.int32)[None, :]).astype(jnp.int32)
    slot_index = lax.optimization_barrier(jnp.sum((jnp.cumsum(one_hot, axis=0) - one_hot) * one_hot, axis=1))
    token_index = jnp.arange(row_total, dtype=jnp.int32) // TOPK
    capacity = N_EXP * CAP

    def one_expert(expert_id):
        matches = flat_routes == expert_id
        position = jnp.where(matches, slot_index, capacity)
        selected = jnp.zeros((capacity + 1,), jnp.int32).at[position].set(token_index)[:capacity]
        inputs = normed[selected]
        return expert_ffn(inputs, w_gate[expert_id], w_up[expert_id], w_down[expert_id])
    outputs = lax.map(one_expert, jnp.arange(EXPERTS, dtype=jnp.int32))
    row_out = outputs[flat_routes, slot_index]
    expert_sum = lax.optimization_barrier(jnp.sum((row_out * route_weight.reshape(-1, 1)).reshape(TOKENS, TOPK, D), axis=1))
    return (residual + expert_sum).astype(jnp.bfloat16)
```

```python
import functools
import math

import jax
import jax.numpy as jnp
import numpy as np
from jax import lax
from jax.experimental import pallas as pl
from jax.experimental.pallas import tpu as pltpu
from jax.sharding import PartitionSpec as P

D = 3584
HL = 8
DN = 128
DR = 64
DC = 512
DV = 128
TOPK = 2
BLK = 128
SHARE = 448
WIDE = 512
T = 128
NCTX = 8
NEXP = 32
CHUNK = 512
SLOTS = 384
GRID = 512
FFL = 128
MESH = pl.DeviceIdType.MESH
F32 = jnp.float32
BF16 = jnp.bfloat16
NT = (((1,), (1,)), ((), ()))
NN = (((1,), (0,)), ((), ()))
NEG = -1e30
AKV = 32
PKG = 144


def dot(a, b, dims=NN):
    return lax.dot_general(a, b, dims, preferred_element_type=F32)


def remote(src, dst, send, recv, **where):
    return pltpu.make_async_remote_copy(
        src_ref=src, dst_ref=dst, send_sem=send, recv_sem=recv, device_id=where, device_id_type=MESH
    )


def place():
    c, e = lax.axis_index("ctx"), lax.axis_index("exp")
    x, y = c // 2, c % 2
    return c, e, x, y


class Around:
    def __init__(self, x, y):
        self.x, self.y = x, y

    def at(self, dx, flip):
        yy = 1 - self.y if flip else self.y
        return ((self.x + dx + 4) % 4) * 2 + yy


class Gather:
    def __init__(self, buf, rows, send, recv, around):
        self.buf, self.rows, self.send, self.recv, self.a = buf, rows, send, recv, around
        self.me = around.at(0, False)
        self.to = {"y": around.at(0, True), "r": around.at(1, False), "l": around.at(-1, False)}

    def op(self, i):
        a, half = self.a, self.rows // 2
        table = [
            ((0, False), (0, True), "y", 0, self.rows),
            ((0, False), (-1, False), "r", 0, self.rows),
            ((0, False), (1, False), "l", 0, self.rows),
            ((0, True), (-1, True), "r", 0, self.rows),
            ((0, True), (1, True), "l", 0, self.rows),
            ((-1, False), (2, False), "r", 0, half),
            ((1, False), (2, False), "l", half, half),
            ((2, False), (2, True), "y", 0, self.rows),
        ]
        src, got, to, first, rows = table[i]
        return a.at(*src), a.at(*got), self.to[to], pl.ds(first, rows)

    def start(self, i, src=None):
        block, _, to, rows = self.op(i)
        here = self.buf.at[block, rows]
        remote(here if src is None else src, here, self.send.at[i], self.recv.at[i], ctx=to).start()

    def arrived(self, i):
        _, block, to, rows = self.op(i)
        here = self.buf.at[block, rows]
        remote(here, here, self.send.at[i], self.recv.at[i], ctx=to).wait_recv()

    def finish(self):
        for i in range(8):
            block, _, to, rows = self.op(i)
            here = self.buf.at[block, rows]
            remote(here, here, self.send.at[i], self.recv.at[i], ctx=to).wait_send()


def greet(peers):
    barrier = pltpu.get_barrier_semaphore()
    for where in peers:
        pl.semaphore_signal(barrier, inc=1, device_id=where, device_id_type=MESH)
    pl.semaphore_wait(barrier, len(peers))


def attention_kernel(
    pkg_ref,
    lat_ref,
    qn_ref,
    qr_ref,
    mask_ref,
    hid_ref,
    out_ref,
    gath,
    latb,
    qlat,
    bias,
    acc,
    mmax,
    lsum,
    attn,
    parts,
    got,
    own_sem,
    w_send,
    w_recv,
    l_send,
    l_recv,
    r_send,
    r_recv,
    *,
    scale,
):
    c, e, x, y = place()
    z, h, k = e // 4, (e // 2) % 2, e % 2
    around = Around(x, y)

    def eid(zz, hh, kk):
        return ((zz + 16) % 8) * 4 + hh * 2 + kk

    up, down = eid(z + 1, h, k), eid(z - 1, h, k)
    partner, sibling = eid(z, 1 - h, k), eid(z, h, 1 - k)
    greet(
        [{"exp": d} for d in (up, down, partner, sibling)]
        + [{"ctx": (c + i) % NCTX} for i in range(1, NCTX)]
    )

    rows_of = (pl.ds(0, AKV), pl.ds(AKV, PKG - AKV))

    def slot(off, flip, other=False):
        return eid(z + off, 1 - h if flip else h, 1 - k if other else k)

    def wcopy(p, ident, block, to, src=None):
        here = gath.at[block, rows_of[p]]
        return remote(
            here if src is None else src.at[rows_of[p]],
            here,
            w_send.at[p, ident],
            w_recv.at[p, ident],
            exp=to,
        )

    def ring_id(sign, off, flip):
        if off == 4:
            return 7 if sign > 0 else 14
        return (1 if sign > 0 else 8) + (off - 1) * 2 + int(flip)

    def sib_id(off, flip):
        return 16 + (off % 8) * 2 + int(flip)

    started = []

    def send_on(p, off, flip, sign, nxt, src=None):
        block, to = slot(-sign * off, flip), (up if sign > 0 else down)
        ident = ring_id(sign, nxt, flip)
        wcopy(p, ident, block, to, src).start()
        started.append((p, ident, block, to))

    def send_sibling(p, off, flip, src=None):
        block = slot(off, flip)
        wcopy(p, sib_id(off, flip), block, sibling, src).start()
        started.append((p, sib_id(off, flip), block, sibling))

    def weights_first(p):
        wcopy(p, 0, e, partner, pkg_ref).start()
        started.append((p, 0, e, partner))
        for sign in (1, -1):
            send_on(p, 0, False, sign, 1, pkg_ref)
        send_sibling(p, 0, False, pkg_ref)

    def weights_partner(p):
        wcopy(p, 0, slot(0, True), partner).wait_recv()
        for sign in (1, -1):
            send_on(p, 0, True, sign, 1)
        send_sibling(p, 0, True)

    def weights_ring(p, off, flip):
        for sign in (1, -1):
            if off == 4 and flip != (sign < 0):
                continue
            wcopy(p, ring_id(sign, off, flip), slot(-sign * off, flip), partner).wait_recv()
            if off < 3 or (off == 3 and flip == (sign < 0)):
                send_on(p, off, flip, sign, off + 1)
            send_sibling(p, -sign * off, flip)

    def weights_sibling(p, off):
        for flip in (False, True):
            wcopy(p, sib_id(off, flip), slot(off, flip, True), sibling).wait_recv()

    lat = Gather(latb, DC + DR, l_send, l_recv, around)

    own_pkg = pltpu.make_async_copy(pkg_ref, gath.at[e], own_sem.at[0])
    own_lat = pltpu.make_async_copy(lat_ref, latb.at[c], own_sem.at[1])
    own_pkg.start()
    own_lat.start()
    weights_first(0)
    for i in range(3):
        lat.start(i, lat_ref)
    weights_first(1)

    token = lax.broadcasted_iota(jnp.int32, (T, CHUNK), 0)
    position = lax.broadcasted_iota(jnp.int32, (T, CHUNK), 1)

    def fill(i, carry):
        open_row = mask_ref[pl.ds(i, 1), :] > 0.0
        seen = (position + i * CHUNK) <= (token + (NCTX * CHUNK - T))
        bias[i] = jnp.where(open_row & seen, 1.0, 0.0)
        return carry

    lax.fori_loop(0, NCTX, fill, 0)

    weights_partner(0)
    weights_ring(0, 1, False)
    weights_ring(0, 1, True)
    lat.arrived(0)
    lat.start(3)
    lat.start(4)
    weights_ring(0, 2, False)
    weights_ring(0, 2, True)
    weights_partner(1)
    weights_ring(0, 3, False)
    weights_ring(0, 3, True)
    lat.arrived(1)
    lat.start(5)
    lat.arrived(2)
    lat.start(6)
    weights_ring(0, 4, False)
    weights_ring(0, 4, True)
    own_pkg.wait()
    own_lat.wait()
    for off in range(8):
        weights_sibling(0, off)

    def absorb(head, carry):
        cols = pl.ds(pl.multiple_of(head * DN, DN), DN)
        rows = pl.ds(pl.multiple_of(head * T, T), T)
        weight = gath[:, 0:16, cols].reshape(DC, DN)
        qlat[rows, :] = dot(qn_ref[rows, :], weight, NT).astype(BF16)
        return carry

    lax.fori_loop(0, HL, absorb, 0)

    factor = scale * math.log2(math.e)

    def attend(first, blocks, lo, hi):
        def body(i, carry):
            rows = pl.ds(pl.multiple_of(i * 2 * T, 2 * T), 2 * T)
            ql, qr = qlat[rows, :], qr_ref[rows, :]
            scores = []
            for b in blocks:
                s = dot(ql, latb[b, 0:DC, :], NT) + dot(qr, latb[b, DC : DC + DR, :])
                allowed = bias[b] > 0.0
                allowed = jnp.concatenate([allowed, allowed], axis=0)
                scores.append(jnp.where(allowed, s * factor, NEG))
            top = jnp.max(jnp.maximum(*scores), axis=1, keepdims=True)
            if not first:
                old = mmax[rows, 0:1]
                top = jnp.maximum(old, top)
            probs = [jnp.exp2(s - top) for s in scores]
            total = jnp.sum(probs[0] + probs[1], axis=1, keepdims=True)
            product = sum(
                dot(p.astype(BF16), latb[b, 0:DC, :]) for p, b in zip(probs, blocks, strict=True)
            )
            if not first:
                shrink = jnp.exp2(old - top)
                total = total + lsum[rows, 0:1] * shrink
                product = product + acc[rows, :] * shrink
            mmax[rows, :] = jnp.broadcast_to(top, (2 * T, 128))
            lsum[rows, :] = jnp.broadcast_to(total, (2 * T, 128))
            acc[rows, :] = product
            return carry

        lax.fori_loop(lo, hi, body, 0)

    def pair(dx):
        return [around.at(dx, False), around.at(dx, True)]

    attend(True, pair(0), 0, 4)
    weights_ring(1, 1, False)
    lat.arrived(4)
    attend(False, pair(1), 0, 4)
    weights_ring(1, 1, True)
    lat.arrived(5)
    lat.arrived(6)
    lat.start(7)
    lat.arrived(3)
    attend(False, pair(-1), 0, 4)
    weights_ring(1, 2, False)
    lat.arrived(7)
    attend(False, pair(2), 0, 4)
    weights_ring(1, 2, True)
    lat.finish()

    def values(head, carry):
        cols = pl.ds(pl.multiple_of(head * DV, DV), DV)
        rows = pl.ds(pl.multiple_of(head * T, T), T)
        weight = gath[:, 16:32, cols].reshape(DC, DV)
        latent_out = (acc[rows, :] / lsum[rows, 0:1]).astype(BF16)
        attn[:, cols] = dot(latent_out, weight).astype(BF16)
        return carry

    lax.fori_loop(0, HL, values, 0)

    def rcopy(dest, source):
        return remote(parts.at[dest], got.at[source], r_send.at[dest], r_recv.at[source], ctx=dest)

    def project(off):
        weights_sibling(1, off)
        dest = (z + off + 8) % 8
        weight = gath[pl.ds(dest * 4, 4), AKV:PKG, :].reshape(SHARE, HL * DV)
        partial = dot(attn[...], weight, NT)
        parts[dest, :, 0:SHARE] = partial.astype(BF16)
        parts[dest, :, SHARE:WIDE] = jnp.zeros((T, WIDE - SHARE), BF16)

        @pl.when(dest != c)
        def _():
            rcopy(dest, c).start()

        @pl.when(dest == c)
        def _():
            got[c] = parts[dest]

    project(0)
    weights_ring(1, 3, False)
    project(1)
    project(-1)
    weights_ring(1, 3, True)
    project(2)
    project(-2)
    weights_ring(1, 4, False)
    weights_ring(1, 4, True)
    project(3)
    project(-3)
    project(4)

    for i in range(1, NCTX):
        source = (c + i) % NCTX
        remote(
            got.at[source], got.at[source], r_send.at[source], r_recv.at[source], ctx=source
        ).wait_recv()
    total = hid_ref[...].astype(F32)
    for i in range(NCTX):
        total = total + got[i, :, 0:SHARE].astype(F32)
    out_ref[...] = total

    for p, ident, block, to in started:
        wcopy(p, ident, block, to).wait_send()
    for i in range(1, NCTX):
        dest = (c + i) % NCTX
        rcopy(dest, c).wait_send()


def expert_kernel(
    r_ref,
    gain_ref,
    place_row_ref,
    place_col_ref,
    weight_ref,
    perm_ref,
    unperm_ref,
    wg_hbm,
    wu_hbm,
    wd_hbm,
    out_ref,
    wg,
    wu,
    wd,
    xs,
    rx,
    xa,
    gate,
    up,
    tails,
    act,
    pd,
    t0,
    t1,
    t2,
    t3,
    t4,
    t5,
    t6,
    t7,
    ys,
    back,
    own_sem,
    a_send,
    a_recv,
    g_send,
    g_recv,
    s_send,
    s_recv,
    b_send,
    b_recv,
):
    c, e, x, y = place()
    around = Around(x, y)
    weights = [
        pltpu.make_async_copy(src, dst, own_sem.at[i])
        for i, (src, dst) in enumerate(((wg_hbm, wg), (wu_hbm, wu), (wd_hbm, wd)))
    ]
    for w in weights:
        w.start()

    barrier = pltpu.get_barrier_semaphore()

    def hello(i, carry):
        pl.semaphore_signal(
            barrier, inc=1, device_id={"exp": (e + i) % NEXP}, device_id_type=MESH
        )
        return carry

    lax.fori_loop(1, NEXP, hello, 0)
    for i in range(1, NCTX):
        pl.semaphore_signal(
            barrier, inc=1, device_id={"ctx": (c + i) % NCTX}, device_id_type=MESH
        )

    resid = r_ref[...]
    squares = jnp.sum(resid * resid, axis=1, keepdims=True)
    high = squares.astype(BF16).astype(F32)
    low = squares - high
    lane = lax.broadcasted_iota(jnp.int32, (T, WIDE - SHARE), 1)
    tail = jnp.where(lane == 0, high, jnp.where(lane == 1, low, 0.0))
    scaled = jnp.concatenate([resid * gain_ref[...], tail], axis=1).astype(BF16)
    where = lax.broadcasted_iota(jnp.int32, (GRID, T), 0)
    chosen = (where == place_row_ref[0:1, :]) | (where == place_row_ref[1:2, :])
    xs[...] = dot(jnp.where(chosen, 1.0, 0.0).astype(BF16), scaled).astype(BF16)

    pl.semaphore_wait(barrier, NEXP - 1 + NCTX - 1)

    def rows16(i):
        return pl.ds(pl.multiple_of(i * 16, 16), 16)

    def exchange(src, dst, send, recv):
        def make(i):
            to = (e + i) % NEXP
            return remote(src.at[rows16(to)], dst.at[rows16(e)], send.at[i], recv.at[i], exp=to)

        def go(i, carry):
            make(i).start()
            return carry

        def land(i, carry):
            frm = (e + NEXP - i) % NEXP
            remote(
                dst.at[rows16(frm)], dst.at[rows16(frm)], send.at[i], recv.at[i], exp=frm
            ).wait_recv()
            return carry

        def left(i, carry):
            make(i).wait_send()
            return carry

        lax.fori_loop(1, NEXP, go, 0)
        dst[rows16(e), :] = src[rows16(e), :]
        lax.fori_loop(1, NEXP, land, 0)
        return lambda: lax.fori_loop(1, NEXP, left, 0)

    a_left = exchange(xs, rx, a_send, a_recv)
    xa[c] = dot(perm_ref[...], rx[...]).astype(BF16)

    ga = Gather(xa, SLOTS, g_send, g_recv, around)
    for i in range(3):
        ga.start(i)

    def feed(block, first=False):
        rows_c = pl.ds(pl.multiple_of(block * SHARE, SHARE), SHARE)

        def body(j, carry):
            rows = pl.ds(pl.multiple_of(j * 96, 96), 96)
            lhs = xa[block, rows, 0:SHARE]
            g = dot(lhs, wg[j, rows_c, :])
            u = dot(lhs, wu[j, rows_c, :])
            t = xa[block, rows, 384:WIDE].astype(F32)
            if first:
                gate[rows, :], up[rows, :], tails[rows, :] = g, u, t
            else:
                gate[rows, :] += g
                up[rows, :] += u
                tails[rows, :] += t
            return carry

        lax.fori_loop(0, 4, body, 0)

    for w in weights:
        w.wait()
    feed(c, True)
    ga.arrived(0)
    ga.start(3)
    ga.start(4)
    feed(around.at(0, True))
    ga.arrived(1)
    ga.start(5)
    ga.arrived(2)
    ga.start(6)
    feed(around.at(-1, False))
    feed(around.at(1, False))
    ga.arrived(5)
    ga.arrived(6)
    ga.start(7)
    feed(around.at(2, False))
    ga.arrived(3)
    feed(around.at(-1, True))
    ga.arrived(4)
    feed(around.at(1, True))
    ga.arrived(7)
    feed(around.at(2, True))
    ga.finish()
    a_left()

    lanes = lax.broadcasted_iota(jnp.int32, (SLOTS, 128), 1)
    kept = jnp.where((lanes == 64) | (lanes == 65), tails[...], 0.0)
    inv = lax.rsqrt(jnp.sum(kept, axis=1, keepdims=True) / D + 1e-06)
    gv = gate[...] * inv
    act[...] = (gv / (1.0 + jnp.exp(-gv)) * (up[...] * inv)).astype(BF16)

    def produce(xx):
        cols = pl.ds(pl.multiple_of(xx * 2 * SHARE, 2 * SHARE), 2 * SHARE)

        def body(j, carry):
            rows = pl.ds(pl.multiple_of(j * 96, 96), 96)
            both = dot(act[rows, :], wd[j, :, cols]).astype(BF16)
            pd[xx * 2, rows, 0:SHARE] = both[:, 0:SHARE]
            pd[xx * 2 + 1, rows, 0:SHARE] = both[:, SHARE:]
            pd[xx * 2, rows, SHARE:WIDE] = jnp.zeros((96, WIDE - SHARE), BF16)
            pd[xx * 2 + 1, rows, SHARE:WIDE] = jnp.zeros((96, WIDE - SHARE), BF16)
            return carry

        lax.fori_loop(0, 4, body, 0)

    half = SLOTS // 2
    lo, hi, whole = pl.ds(0, half), pl.ds(half, half), pl.ds(0, SLOTS)
    yp, xr, xl = around.at(0, True), around.at(1, False), around.at(-1, False)
    sends = [
        (around.at(2, True), whole, t0, yp),
        (around.at(1, True), whole, t1, xr),
        (around.at(-1, True), whole, t2, xl),
        (around.at(2, False), lo, t3, xr),
        (around.at(2, False), hi, t4, xl),
        (around.at(0, True), whole, t5, yp),
        (around.at(1, False), hi, t6.at[hi], xr),
        (around.at(-1, False), lo, t7.at[lo], xl),
        (around.at(1, False), lo, t6.at[lo], xr),
        (around.at(-1, False), hi, t7.at[hi], xl),
    ]

    def scopy(i):
        block, rows, dst, to = sends[i]
        return remote(pd.at[block, rows], dst, s_send.at[i], s_recv.at[i], ctx=to)

    def sgot(i):
        _, _, dst, to = sends[i]
        remote(dst, dst, s_send.at[i], s_recv.at[i], ctx=to).wait_recv()

    def add(block, rows, *terms):
        total = pd[block, rows, :].astype(F32)
        for t in terms:
            total = total + t[...].astype(F32)
        pd[block, rows, :] = total.astype(BF16)

    produce((x + 2) % 4)
    scopy(0).start()
    produce((x + 1) % 4)
    scopy(1).start()
    scopy(6).start()
    produce((x + 3) % 4)
    scopy(2).start()
    scopy(7).start()
    sgot(0)
    add(around.at(2, False), whole, t0)
    scopy(3).start()
    scopy(4).start()
    produce(x)
    sgot(1)
    sgot(2)
    add(around.at(0, True), whole, t1, t2)
    scopy(5).start()
    sgot(3)
    add(around.at(1, False), lo, t3)
    scopy(8).start()
    sgot(4)
    add(around.at(-1, False), hi, t4)
    scopy(9).start()
    for i in (5, 6, 7, 8, 9):
        sgot(i)
    total = pd[c].astype(F32)
    for t in (t5, t6, t7):
        total = total + t[...].astype(F32)
    ys[...] = dot(unperm_ref[...], total.astype(BF16)).astype(BF16)

    b_left = exchange(ys, back, b_send, b_recv)
    spots = lax.broadcasted_iota(jnp.int32, (T, GRID), 1)
    result = resid
    for kk in range(TOPK):
        picked = jnp.where(spots == place_col_ref[:, kk : kk + 1], 1.0, 0.0).astype(BF16)
        result = result + dot(picked, back[...])[:, 0:SHARE] * weight_ref[:, kk : kk + 1]
    out_ref[...] = result.astype(BF16)

    for i in range(10):
        scopy(i).wait_send()
    b_left()


def permutations():
    perm = np.zeros((SLOTS, GRID), np.float32)
    for j in range(4):
        for s in range(NEXP):
            for i in range(3):
                perm[j * 96 + s * 3 + i, s * 16 + j * 4 + i] = 1.0
    return perm


VMEM = pl.BlockSpec(memory_space=pltpu.VMEM)
ANY = pl.BlockSpec(memory_space=pl.ANY)


def local(
    query,
    latent_cache,
    absorb_key,
    absorb_value,
    out_weight,
    hidden,
    norm_gain,
    block_mask,
    routes,
    route_weight,
    w_gate,
    w_up,
    w_down,
):
    ctx_index = lax.axis_index("ctx")
    scale = 1.0 / math.sqrt(DN + DR)
    pkg = jnp.concatenate(
        [
            absorb_key.transpose(2, 0, 1).reshape(16, HL * DN),
            absorb_value.transpose(1, 0, 2).reshape(16, HL * DV),
            out_weight.T,
        ],
        axis=0,
    )
    latent = jnp.concatenate([latent_cache[0, :, :DC], latent_cache[0, :, DC:].T], axis=0)
    queries = query.reshape(T, HL, DN + DR).transpose(1, 0, 2).reshape(HL * T, DN + DR)
    mask = jnp.repeat(block_mask[-1].astype(F32), BLK).reshape(NCTX, CHUNK)

    flat = routes.reshape(-1)
    one_hot = (flat[:, None] == jnp.arange(128, dtype=jnp.int32)[None, :]).astype(BF16)
    before = jnp.tril(jnp.ones((T * TOPK, T * TOPK), BF16), -1)
    count = jnp.dot(before, one_hot, preferred_element_type=F32)
    slot = jnp.sum(count * one_hot.astype(F32), axis=1).astype(jnp.int32)
    places = (flat * 4 + slot).reshape(T, TOPK)
    place_row = jnp.concatenate([places.T, jnp.full((6, T), -1, jnp.int32)], axis=0)
    gain = lax.dynamic_slice_in_dim(norm_gain, ctx_index * SHARE, SHARE, 0)[None, :]

    residual = pl.pallas_call(
        functools.partial(attention_kernel, scale=scale),
        out_shape=jax.ShapeDtypeStruct((T, SHARE), F32),
        in_specs=[ANY, ANY, VMEM, VMEM, VMEM, VMEM],
        out_specs=VMEM,
        scratch_shapes=[
            pltpu.VMEM((NEXP, PKG, HL * DV), BF16),
            pltpu.VMEM((NCTX, DC + DR, CHUNK), BF16),
            pltpu.VMEM((HL * T, DC), BF16),
            pltpu.VMEM((NCTX, T, CHUNK), F32),
            pltpu.VMEM((HL * T, DC), F32),
            pltpu.VMEM((HL * T, 128), F32),
            pltpu.VMEM((HL * T, 128), F32),
            pltpu.VMEM((T, HL * DV), BF16),
            pltpu.VMEM((NCTX, T, WIDE), BF16),
            pltpu.VMEM((NCTX, T, WIDE), BF16),
            pltpu.SemaphoreType.DMA((2,)),
            pltpu.SemaphoreType.DMA((2, 32)),
            pltpu.SemaphoreType.DMA((2, 32)),
            pltpu.SemaphoreType.DMA((8,)),
            pltpu.SemaphoreType.DMA((8,)),
            pltpu.SemaphoreType.DMA((8,)),
            pltpu.SemaphoreType.DMA((8,)),
        ],
        compiler_params=pltpu.CompilerParams(
            collective_id=0, has_side_effects=True, vmem_limit_bytes=48 * 1024 * 1024
        ),
        name="attention",
    )(pkg, latent, queries[:, :DN], queries[:, DN:], mask, hidden)

    perm = permutations()
    dma = pltpu.SemaphoreType.DMA
    return pl.pallas_call(
        expert_kernel,
        out_shape=jax.ShapeDtypeStruct((T, SHARE), BF16),
        in_specs=[VMEM] * 7 + [ANY] * 3,
        out_specs=VMEM,
        scratch_shapes=[
            pltpu.VMEM((4, D, FFL), BF16),
            pltpu.VMEM((4, D, FFL), BF16),
            pltpu.VMEM((4, FFL, D), BF16),
            pltpu.VMEM((GRID, WIDE), BF16),
            pltpu.VMEM((GRID, WIDE), BF16),
            pltpu.VMEM((NCTX, SLOTS, WIDE), BF16),
            pltpu.VMEM((SLOTS, FFL), F32),
            pltpu.VMEM((SLOTS, FFL), F32),
            pltpu.VMEM((SLOTS, 128), F32),
            pltpu.VMEM((SLOTS, FFL), BF16),
            pltpu.VMEM((NCTX, SLOTS, WIDE), BF16),
            pltpu.VMEM((SLOTS, WIDE), BF16),
            pltpu.VMEM((SLOTS, WIDE), BF16),
            pltpu.VMEM((SLOTS, WIDE), BF16),
            pltpu.VMEM((SLOTS // 2, WIDE), BF16),
            pltpu.VMEM((SLOTS // 2, WIDE), BF16),
            pltpu.VMEM((SLOTS, WIDE), BF16),
            pltpu.VMEM((SLOTS, WIDE), BF16),
            pltpu.VMEM((SLOTS, WIDE), BF16),
            pltpu.VMEM((GRID, WIDE), BF16),
            pltpu.VMEM((GRID, WIDE), BF16),
            dma((3,)),
            dma((32,)),
            dma((32,)),
            dma((8,)),
            dma((8,)),
            dma((10,)),
            dma((10,)),
            dma((32,)),
            dma((32,)),
        ],
        compiler_params=pltpu.CompilerParams(
            collective_id=1, has_side_effects=True, vmem_limit_bytes=48 * 1024 * 1024
        ),
        name="experts",
    )(
        residual,
        gain,
        place_row,
        places,
        route_weight,
        jnp.asarray(perm, BF16),
        jnp.asarray(perm.T, BF16),
        w_gate,
        w_up,
        w_down,
    )


def solution(mesh):
    in_specs = (
        P("exp", "ctx"),
        P("exp", "ctx", None),
        P("ctx", None, "exp"),
        P("ctx", "exp", None),
        P("ctx", "exp"),
        P("exp", "ctx"),
        P(),
        P(),
        P("exp", None),
        P("exp", None),
        P("exp", None, "ctx"),
        P("exp", None, "ctx"),
        P("exp", "ctx", None),
    )
    out_specs = P("exp", "ctx")
    return jax.shard_map(local, mesh=mesh, in_specs=in_specs, out_specs=out_specs, check_vma=False)
```

```python
import functools
import math

import jax
import jax.numpy as jnp
import numpy as np
from jax import lax
from jax.experimental import pallas as pl
from jax.experimental.pallas import tpu as pltpu
from jax.sharding import PartitionSpec as P

D = 3584
HL = 8
DN = 128
DR = 64
DC = 512
DV = 128
TOPK = 2
BLK = 128
SHARE = 448
WIDE = 512
T = 128
NCTX = 8
NEXP = 32
CHUNK = 512
SLOTS = 384
GRID = 512
FFL = 128
MESH = pl.DeviceIdType.MESH
F32 = jnp.float32
BF16 = jnp.bfloat16
NT = (((1,), (1,)), ((), ()))
NN = (((1,), (0,)), ((), ()))
NEG = -1e38
WO = 112
ROWS = 96
MASKED = DC + DR
CAUSAL = MASKED + 16
DEPTH = CAUSAL + T
HALF_LAT = (DC + DR) // 2
PIECE_ROWS = {1: (0, 32), 2: (32, 32), 4: (64, 48), 5: (0, WO)}
LAST_PIECE = 4

PLAN = (
    ("first", 0), ("latents", 0), ("latents", 1), ("first", 1), ("first", 2), ("prepare",), ("ring", 0, 1, 0),
    ("partner", 0), ("first", 4), ("ring", 0, 2, 0), ("ring", 0, 1, 1), ("ring", 1, 1, 0), ("first", 3),
    ("halves", 0), ("spread", 0), ("ring", 0, 3, 0), ("ring", 0, 2, 1), ("ring", 2, 1, 0), ("ring", 1, 2, 0),
    ("ring", 0, 3, 1), ("ring", 3, 1, 0), ("ring", 4, 1, 0), ("halves", 1), ("ring", 2, 2, 0), ("spread", 1),
    ("ring", 1, 3, 0), ("partner", 1), ("far", 0), ("cross", 0), ("partner", 2), ("absorb",), ("partner", 3),
    ("partner", 4), ("attend", 0, 0), ("ring", 3, 2, 0), ("attend", 0, 1), ("ring", 1, 1, 1),
    ("ring", 4, 2, 0), ("attend", 0, 2), ("attend", 0, 3), ("cross", 1), ("ring", 2, 1, 1), ("attend", 1, 0),
    ("ring", 3, 1, 1), ("ring", 4, 1, 1), ("attend", 1, 1), ("ring", 1, 2, 1), ("attend", 1, 2),
    ("ring", 2, 3, 0), ("attend", 1, 3), ("ring", 2, 2, 1), ("attend", 2, 0), ("ring", 3, 2, 1),
    ("ring", 3, 3, 0), ("attend", 2, 1), ("ring", 4, 2, 1), ("attend", 2, 2), ("ring", 4, 3, 0),
    ("attend", 2, 3), ("attend", 3, 0), ("ring", 1, 3, 1), ("ring", 2, 3, 1), ("ring", 3, 3, 1),
    ("attend", 3, 1), ("attend", 3, 2), ("ring", 4, 3, 1), ("attend", 3, 3), ("far", 1), ("far", 2),
    ("far", 3), ("far", 4), ("values",), ("project", 0), ("project", 1), ("project", -1), ("project", 2),
    ("project", -2), ("project", 3), ("project", -3), ("project", 4),
)


def dot(a, b, dims=NN):
    return lax.dot_general(a, b, dims, preferred_element_type=F32)


def remote(src, dst, send, recv, **where):
    return pltpu.make_async_remote_copy(
        src_ref=src, dst_ref=dst, send_sem=send, recv_sem=recv, device_id=where, device_id_type=MESH
    )


def place():
    c, e = lax.axis_index("ctx"), lax.axis_index("exp")
    x, y = c // 2, c % 2
    return c, e, x, y


class Around:
    def __init__(self, x, y):
        self.x, self.y = x, y

    def at(self, dx, flip):
        yy = 1 - self.y if flip else self.y
        return ((self.x + dx + 4) % 4) * 2 + yy


class Gather:
    def __init__(self, view, rows, send, recv, around):
        self.view, self.rows, self.send, self.recv, self.a = view, rows, send, recv, around
        self.to = {"y": around.at(0, True), "r": around.at(1, False), "l": around.at(-1, False)}

    def op(self, i):
        a, half = self.a, self.rows // 2
        table = [
            ((0, False), (0, True), "y", 0, self.rows),
            ((0, False), (-1, False), "r", 0, self.rows),
            ((0, False), (1, False), "l", 0, self.rows),
            ((0, True), (-1, True), "r", 0, self.rows),
            ((0, True), (1, True), "l", 0, self.rows),
            ((-1, False), (2, False), "r", 0, half),
            ((1, False), (2, False), "l", half, half),
            ((2, False), (2, True), "y", 0, self.rows),
        ]
        src, got, to, first, rows = table[i]
        return a.at(*src), a.at(*got), self.to[to], first, rows

    def copy(self, i, arriving=False, src=None):
        block, got, to, first, rows = self.op(i)
        here = self.view(got if arriving else block, first, rows)
        return remote(here if src is None else src, here, self.send.at[i], self.recv.at[i], ctx=to)

    def start(self, i, src=None):
        self.copy(i, src=src).start()

    def arrived(self, *ops):
        for i in ops:
            self.copy(i, arriving=True).wait_recv()

    def first(self):
        for i in range(3):
            self.start(i)

    def spread(self):
        self.arrived(0)
        self.start(3)
        self.start(4)

    def halves(self):
        self.arrived(1)
        self.start(5)
        self.arrived(2)
        self.start(6)

    def cross(self):
        self.arrived(5, 6)
        self.start(7)

    def finish(self):
        for i in range(8):
            self.copy(i).wait_send()


def layer_kernel(
    q_ref,
    lat_ref,
    ak_ref,
    av_ref,
    wo_ref,
    hid_ref,
    gain_ref,
    mask_ref,
    routes_ref,
    weight_ref,
    perm_ref,
    unperm_ref,
    wg_hbm,
    wu_hbm,
    wd_hbm,
    out_ref,
    gak,
    gav,
    gwo,
    latb,
    qlat,
    sbuf,
    acc,
    mmax,
    lsum,
    attn,
    parts,
    got,
    qb,
    hidb,
    perm,
    unperm,
    wg,
    wu,
    wd,
    xs,
    rx,
    xa,
    pd,
    tb,
    fin,
    ys,
    back,
    own_sem,
    w_send,
    w_recv,
    l_send,
    l_recv,
    r_send,
    r_recv,
    a_send,
    a_recv,
    g_send,
    g_recv,
    s_send,
    s_recv,
    b_send,
    b_recv,
    *,
    scale,
):
    c, e, x, y = place()
    z, h, k = e // 4, (e // 2) % 2, e % 2
    around = Around(x, y)

    def eid(zz, hh, kk):
        return ((zz + 16) % 8) * 4 + hh * 2 + kk

    up, down = eid(z + 1, h, k), eid(z - 1, h, k)
    partner, sibling = eid(z, 1 - h, k), eid(z, h, 1 - k)

    local_copies = [
        pltpu.make_async_copy(src, dst, own_sem.at[i])
        for i, (src, dst) in enumerate(
            (
                (ak_ref, gak.at[e]),
                (lat_ref, latb.at[c, pl.ds(0, MASKED)]),
                (av_ref, gav.at[e]),
                (wo_ref, gwo.at[e]),
                (wg_hbm, wg),
                (wu_hbm, wu),
                (wd_hbm, wd),
                (q_ref, qb),
                (hid_ref, hidb),
                (perm_ref, perm),
                (unperm_ref, unperm),
            )
        )
    ]
    for copy in local_copies[:4] + local_copies[7:8]:
        copy.start()

    barrier = pltpu.get_barrier_semaphore()

    def hello(i, carry):
        pl.semaphore_signal(
            barrier, inc=1, device_id={"exp": (e + i) % NEXP}, device_id_type=MESH
        )
        return carry

    lax.fori_loop(1, NEXP, hello, 0)
    for i in range(1, NCTX):
        pl.semaphore_signal(
            barrier, inc=1, device_id={"ctx": (c + i) % NCTX}, device_id_type=MESH
        )
    pl.semaphore_wait(barrier, NEXP - 1 + NCTX - 1)


    def piece(p, block):
        if p == 0:
            return gak.at[block]
        if p == 3:
            return gav.at[block]
        return gwo.at[block, pl.ds(*PIECE_ROWS[p])]

    def own_piece(p):
        if p == 0:
            return ak_ref
        if p == 3:
            return av_ref
        return wo_ref.at[pl.ds(*PIECE_ROWS[p])]

    def slot(off, flip, other=False):
        return eid(z + off, 1 - h if flip else h, 1 - k if other else k)

    def wcopy(p, ident, block, to, own=False):
        here = piece(p, block)
        return remote(
            own_piece(p) if own else here, here, w_send.at[p, ident], w_recv.at[p, ident], exp=to
        )

    def ring_id(sign, off, flip):
        if off == 4:
            return 7 if sign > 0 else 14
        return (1 if sign > 0 else 8) + (off - 1) * 2 + int(flip)

    def sib_id(off, flip):
        return 16 + (off % 8) * 2 + int(flip)

    started = []

    def send(p, ident, off, flip, to, own=False):
        wcopy(p, ident, slot(off, flip), to, own).start()
        started.append((p, ident, off, flip, to))

    def send_on(p, off, flip, sign, own=False):
        ident = ring_id(sign, off + 1, flip)
        send(p, ident, -sign * off, flip, up if sign > 0 else down, own)

    def send_sibling(p, off, flip, own=False):
        if p == LAST_PIECE:
            p = 5
        if p in (0, 3, 5):
            send(p, sib_id(off, flip), off, flip, sibling, own)

    def weights_first(p):
        for sign in (1, -1):
            send_on(p, 0, False, sign, True)
        send(p, 0, 0, False, partner, True)
        send_sibling(p, 0, False, True)

    def weights_partner(p):
        wcopy(p, 0, slot(0, True), partner).wait_recv()
        for sign in (1, -1):
            send_on(p, 0, True, sign)
        send_sibling(p, 0, True)

    def weights_ring(p, off, flip):
        for sign in (1, -1):
            wcopy(p, ring_id(sign, off, flip), slot(-sign * off, flip), partner).wait_recv()
        for sign in (1, -1):
            if off < 3 or flip == (sign < 0):
                send_on(p, off, flip, sign)
            send_sibling(p, -sign * off, flip)

    def weights_far(p):
        for sign in (1, -1):
            flip = sign < 0
            wcopy(p, ring_id(sign, 4, flip), slot(4, flip), partner).wait_recv()
        for flip in (False, True):
            send_sibling(p, 4, flip)

    def weights_sibling(off, *ps):
        for p in ps:
            for flip in (False, True):
                wcopy(p, sib_id(off, flip), slot(off, flip, True), sibling).wait_recv()

    def latent_view(base):
        return lambda block, first, rows: latb.at[block, pl.ds(base + first, rows)]

    lats = [
        Gather(latent_view(i * HALF_LAT), HALF_LAT, l_send.at[i], l_recv.at[i], around)
        for i in range(2)
    ]

    def latents_first(i):
        for op in range(3):
            lats[i].start(op, lat_ref.at[pl.ds(i * HALF_LAT, HALF_LAT)])

    def prepare():
        for copy in local_copies[4:7] + local_copies[8:]:
            copy.start()
        top = lax.broadcasted_iota(jnp.int32, (16, BLK), 0) == 0

        def fill(i, carry):
            for b in range(CHUNK // BLK):
                cols = slice(b * BLK, (b + 1) * BLK)
                is_open = mask_ref[NCTX * CHUNK // BLK - 1, i * (CHUNK // BLK) + b].astype(F32)
                taken = jnp.where(top, NEG, 0.0) * (1.0 - is_open)
                latb[i, MASKED:CAUSAL, cols] = taken.astype(BF16)
            latb[i, CAUSAL:DEPTH, :] = jnp.zeros((T, CHUNK), BF16)
            return carry

        lax.fori_loop(0, NCTX, fill, 0)
        latb[NCTX - 1, CAUSAL:DEPTH, CHUNK - T : CHUNK] = jnp.where(lane > sub, NEG, 0.0).astype(BF16)
        ones = jnp.where(lane[:, 0:16] == 0, 1.0, 0.0).astype(BF16)
        for head in range(HL):
            qlat[head * T : (head + 1) * T, MASKED:CAUSAL] = ones
            qlat[head * T : (head + 1) * T, CAUSAL:DEPTH] = eye

    sub = lax.broadcasted_iota(jnp.int32, (T, T), 0)
    lane = lax.broadcasted_iota(jnp.int32, (T, T), 1)
    eye = jnp.where(sub == lane, 1.0, 0.0).astype(BF16)

    def column(row):
        return jnp.sum(jnp.where(sub == lane, row, 0.0), axis=1, keepdims=True)

    def places():
        earlier = jnp.where(sub < lane, 1.0, 0.0).astype(BF16)
        expert_of_row = sub.astype(F32)
        routes = [routes_ref[i : i + 1, :].astype(F32) for i in range(TOPK)]
        named = [jnp.where(expert_of_row == r, 1.0, 0.0) for r in routes]
        before = dot((named[0] + named[1]).astype(BF16), earlier)
        return [
            r * 4 + jnp.sum(before * n, axis=0, keepdims=True)
            for r, n in zip(routes, named, strict=True)
        ]

    def absorb():
        for off in range(8):
            weights_sibling(off, 0)
        for copy in local_copies[:4] + local_copies[7:8]:
            copy.wait()

        def body(i, carry):
            pair_q = qb[:, pl.ds(pl.multiple_of(i * 384, 384), 384)]
            for j in range(2):
                at = j * (DN + DR)
                rows = pl.ds(pl.multiple_of(i * 2 * T + j * T, T), T)
                weight = gak[:, pl.ds(i * 2 + j, 1)].reshape(DC, DN)
                qlat[rows, 0:DC] = (dot(pair_q[:, at : at + DN], weight, NT) * factor).astype(BF16)
                rope = pair_q[:, at + DN : at + DN + DR].astype(F32) * factor
                qlat[rows, DC : DC + DR] = rope.astype(BF16)
            return carry

        lax.fori_loop(0, HL // 2, body, 0)

    factor = scale * math.log2(math.e)
    groups = [
        [around.at(0, False), around.at(0, True)],
        [around.at(-1, False), around.at(1, False)],
        [around.at(2, False), around.at(-1, True)],
        [around.at(1, True), around.at(2, True)],
    ]
    step_rows = HL * T // 4

    def score(g, q):
        rows = pl.ds(q * step_rows, step_rows)
        for i, b in enumerate(groups[g]):
            sbuf[q % 2, i] = dot(qlat[rows, :], latb[b])

    def attend(g, q):
        if q == 0:
            for piece_of in lats:
                if g == 2:
                    piece_of.arrived(3)
                if g == 3:
                    piece_of.arrived(4, 7)
            score(g, 0)
        if q < 3:
            score(g, q + 1)
        rows = pl.ds(q * step_rows, step_rows)
        scores = [sbuf[q % 2, i] for i in range(2)]
        top = jnp.max(jnp.maximum(*scores), axis=1, keepdims=True)
        if g > 0:
            old = mmax[rows, 0:1]
            top = jnp.maximum(old, top)
        probs = [jnp.exp2(s - top) for s in scores]
        total = jnp.sum(probs[0] + probs[1], axis=1, keepdims=True)
        product = sum(
            dot(p.astype(BF16), latb[b, 0:DC, :], NT)
            for p, b in zip(probs, groups[g], strict=True)
        )
        if g > 0:
            shrink = jnp.exp2(old - top)
            total = total + lsum[rows, 0:1] * shrink
            product = product + acc[rows, :] * shrink
        mmax[rows, :] = jnp.broadcast_to(top, (step_rows, 128))
        lsum[rows, :] = jnp.broadcast_to(total, (step_rows, 128))
        acc[rows, :] = product

    def values():
        for off in range(8):
            weights_sibling(off, 3)

        def body(head, carry):
            cols = pl.ds(pl.multiple_of(head * DV, DV), DV)
            rows = pl.ds(pl.multiple_of(head * T, T), T)
            weight = gav[:, pl.ds(head, 1)].reshape(DC, DV)
            latent_out = (acc[rows, :] * (1.0 / lsum[rows, 0:1])).astype(BF16)
            attn[:, cols] = dot(latent_out, weight).astype(BF16)
            return carry

        lax.fori_loop(0, HL, body, 0)


    def rcopy(dest, source):
        return remote(parts.at[dest], got.at[source], r_send.at[dest], r_recv.at[source], ctx=dest)

    def project(off):
        weights_sibling(off, 5)
        dest = (z + off + 8) % 8
        weight = gwo[pl.ds(dest * 4, 4)].reshape(SHARE, HL * DV)
        partial = dot(attn[...], weight, NT)
        parts[dest, :, 0:SHARE] = partial.astype(BF16)
        parts[dest, :, SHARE:WIDE] = jnp.zeros((T, WIDE - SHARE), BF16)

        @pl.when(dest != c)
        def _():
            rcopy(dest, c).start()

        @pl.when(dest == c)
        def _():
            got[c] = parts[dest]

    acts = {
        "first": weights_first,
        "partner": weights_partner,
        "ring": weights_ring,
        "far": weights_far,
        "latents": latents_first,
        "spread": lambda i: lats[i].spread(),
        "halves": lambda i: lats[i].halves(),
        "cross": lambda i: lats[i].cross(),
        "prepare": prepare,
        "absorb": absorb,
        "attend": attend,
        "values": values,
        "project": project,
    }
    for act, *how in PLAN:
        acts[act](*how)
    place_rows = places()
    place_cols = [column(r) for r in place_rows]

    for i in range(1, NCTX):
        source = (c + i) % NCTX
        here = got.at[source]
        remote(here, here, r_send.at[source], r_recv.at[source], ctx=source).wait_recv()
    for copy in local_copies[4:7] + local_copies[8:]:
        copy.wait()
    resid = dot(eye, hidb[...], NT)
    for i in range(NCTX):
        resid = resid + got[i, :, 0:SHARE].astype(F32)

    squares = jnp.sum(resid * resid, axis=1, keepdims=True)
    high = squares.astype(BF16).astype(F32)
    low = squares - high
    beside = lax.broadcasted_iota(jnp.int32, (T, WIDE - SHARE), 1)
    tail = jnp.where(beside == 0, high, jnp.where(beside == 1, low, 0.0))
    gains = jnp.concatenate([gain_ref[pl.ds(x * 7 + i, 1), :] for i in range(7)], axis=1)
    gain = jnp.where(y == 0, gains[:, 0:SHARE], gains[:, SHARE:])
    scaled = jnp.concatenate([resid * gain, tail], axis=1).astype(BF16)
    where = lax.broadcasted_iota(jnp.int32, (GRID, T), 0).astype(F32)
    chosen = (where == place_rows[0]) | (where == place_rows[1])
    xs[...] = dot(jnp.where(chosen, 1.0, 0.0).astype(BF16), scaled).astype(BF16)

    def rows16(i):
        return pl.ds(pl.multiple_of(i * 16, 16), 16)

    def exchange(src, dst, send_sem, recv_sem):
        def make(i):
            to = (e + i) % NEXP
            return remote(
                src.at[rows16(to)], dst.at[rows16(e)], send_sem.at[i], recv_sem.at[i], exp=to
            )

        def go(i, carry):
            make(i).start()
            return carry

        def land(i, carry):
            frm = (e + NEXP - i) % NEXP
            here = dst.at[rows16(frm)]
            remote(here, here, send_sem.at[i], recv_sem.at[i], exp=frm).wait_recv()
            return carry

        def left(i, carry):
            make(i).wait_send()
            return carry

        lax.fori_loop(1, NEXP, go, 0)
        dst[rows16(e), :] = src[rows16(e), :]
        lax.fori_loop(1, NEXP, land, 0)
        return lambda: lax.fori_loop(1, NEXP, left, 0)

    a_left = exchange(xs, rx, a_send, a_recv)
    for j in range(4):
        xa[c, j] = dot(perm[j * ROWS : (j + 1) * ROWS, :], rx[...]).astype(BF16)

    def rows_view(j):
        return lambda block, first, rows: xa.at[block, j, pl.ds(first, rows)]

    gathers = [Gather(rows_view(j), ROWS, g_send.at[j], g_recv.at[j], around) for j in range(4)]
    for g in gathers:
        g.first()

    lanes = lax.broadcasted_iota(jnp.int32, (ROWS, 128), 1)

    def expert(j):
        gathers[j].arrived(3, 4, 7)

        def feed(block, carry):
            g, u, t = carry
            rows_c = pl.ds(pl.multiple_of(block * SHARE, SHARE), SHARE)
            lhs = xa[block, j, :, 0:SHARE]
            g = g + dot(lhs, wg[j, rows_c, :])
            u = u + dot(lhs, wu[j, rows_c, :])
            return g, u, t + xa[block, j, :, 384:WIDE].astype(F32)

        zero = jnp.zeros((ROWS, FFL), F32)
        g, u, t = lax.fori_loop(0, NCTX, feed, (zero, zero, zero))
        kept = jnp.where((lanes == 64) | (lanes == 65), t, 0.0)
        inv = lax.rsqrt(jnp.sum(kept, axis=1, keepdims=True) / D + 1e-06)
        g, u = g * inv, u * inv
        act = (g / (1.0 + jnp.exp(-g)) * u).astype(BF16)

        def produce(xx, carry):
            cols = pl.ds(pl.multiple_of(xx * 2 * SHARE, 2 * SHARE), 2 * SHARE)
            both = dot(act, wd[j, :, cols]).astype(BF16)
            blank = jnp.zeros((ROWS, WIDE - SHARE), BF16)
            pd[xx * 2, j, :, 0:SHARE] = both[:, 0:SHARE]
            pd[xx * 2 + 1, j, :, 0:SHARE] = both[:, SHARE:]
            pd[xx * 2, j, :, SHARE:WIDE] = blank
            pd[xx * 2 + 1, j, :, SHARE:WIDE] = blank
            return carry

        lax.fori_loop(0, NCTX // 2, produce, 0)
        for i in (0, 1, 2, 6, 7):
            scopy(j, i).start()

    half = ROWS // 2
    lo, hi, whole = pl.ds(0, half), pl.ds(half, half), pl.ds(0, ROWS)
    yp, xr, xl = around.at(0, True), around.at(1, False), around.at(-1, False)
    sends = [
        (around.at(2, True), whole, 0, yp),
        (around.at(1, True), whole, 1, xr),
        (around.at(-1, True), whole, 2, xl),
        (around.at(2, False), lo, 3, xr),
        (around.at(2, False), hi, 4, xl),
        (around.at(0, True), whole, 5, yp),
        (around.at(1, False), hi, 6, xr),
        (around.at(-1, False), lo, 7, xl),
        (around.at(1, False), lo, 6, xr),
        (around.at(-1, False), hi, 7, xl),
    ]

    def scopy(j, i):
        block, rows, land, to = sends[i]
        return remote(
            pd.at[block, j, rows], tb.at[land, j, rows], s_send.at[j, i], s_recv.at[j, i], ctx=to
        )

    def sgot(j, *ops):
        for i in ops:
            _, rows, land, to = sends[i]
            here = tb.at[land, j, rows]
            remote(here, here, s_send.at[j, i], s_recv.at[j, i], ctx=to).wait_recv()

    def add(j, block, rows, *lands):
        total = pd[block, j, rows, :].astype(F32)
        for land in lands:
            total = total + tb[land, j, rows, :].astype(F32)
        pd[block, j, rows, :] = total.astype(BF16)

    def reduce1(j):
        sgot(j, 0)
        add(j, around.at(2, False), whole, 0)
        scopy(j, 3).start()
        scopy(j, 4).start()
        sgot(j, 1, 2)
        add(j, around.at(0, True), whole, 1, 2)
        scopy(j, 5).start()

    def reduce2(j):
        sgot(j, 3)
        add(j, around.at(1, False), lo, 3)
        scopy(j, 8).start()
        sgot(j, 4)
        add(j, around.at(-1, False), hi, 4)
        scopy(j, 9).start()

    def reduce3(j):
        sgot(j, 5, 6, 7, 8, 9)
        total = pd[c, j].astype(F32)
        for land in (5, 6, 7):
            total = total + tb[land, j].astype(F32)
        fin[j * ROWS : (j + 1) * ROWS, :] = total.astype(BF16)

    gathers[0].spread()
    gathers[0].halves()
    gathers[1].spread()
    gathers[1].halves()
    gathers[0].cross()
    gathers[2].spread()
    gathers[2].halves()
    gathers[3].spread()
    gathers[3].halves()
    gathers[1].cross()
    expert(0)
    gathers[2].cross()
    gathers[3].cross()
    expert(1)
    reduce1(0)
    expert(2)
    reduce1(1)
    reduce2(0)
    expert(3)
    reduce1(2)
    reduce2(1)
    reduce3(0)
    reduce1(3)
    reduce2(2)
    reduce3(1)
    reduce2(3)
    reduce3(2)
    reduce3(3)
    ys[...] = dot(unperm[...], fin[...]).astype(BF16)

    b_left = exchange(ys, back, b_send, b_recv)
    spots = lax.broadcasted_iota(jnp.int32, (T, GRID), 1).astype(F32)
    result = resid
    for i in range(TOPK):
        picked = jnp.where(spots == place_cols[i], 1.0, 0.0).astype(BF16)
        result = result + dot(picked, back[...])[:, 0:SHARE] * column(weight_ref[i : i + 1, :])
    out_ref[...] = result.astype(BF16)

    for p, ident, off, flip, to in started:
        wcopy(p, ident, slot(off, flip), to).wait_send()
    for g in lats + gathers:
        g.finish()
    for i in range(1, NCTX):
        rcopy((c + i) % NCTX, c).wait_send()
    for j in range(4):
        for i in range(10):
            scopy(j, i).wait_send()
    a_left()
    b_left()


def permutations():
    perm = np.zeros((SLOTS, GRID), np.float32)
    for j in range(4):
        for s in range(NEXP):
            for i in range(3):
                perm[j * ROWS + s * 3 + i, s * 16 + j * 4 + i] = 1.0
    return perm


VMEM = pl.BlockSpec(memory_space=pltpu.VMEM)
SMEM = pl.BlockSpec(memory_space=pltpu.SMEM)
ANY = pl.BlockSpec(memory_space=pl.ANY)


def local(
    query,
    latent_cache,
    absorb_key,
    absorb_value,
    out_weight,
    hidden,
    norm_gain,
    block_mask,
    routes,
    route_weight,
    w_gate,
    w_up,
    w_down,
):
    perm = permutations()
    dma = pltpu.SemaphoreType.DMA
    return pl.pallas_call(
        functools.partial(layer_kernel, scale=1.0 / math.sqrt(DN + DR)),
        out_shape=jax.ShapeDtypeStruct((T, SHARE), BF16),
        in_specs=[ANY] * 6 + [VMEM, SMEM, VMEM, VMEM] + [ANY] * 5,
        out_specs=VMEM,
        scratch_shapes=[
            pltpu.VMEM((NEXP, HL, 16, DN), BF16),
            pltpu.VMEM((NEXP, HL, 16, DV), BF16),
            pltpu.VMEM((NEXP, WO, HL * DV), BF16),
            pltpu.VMEM((NCTX, DEPTH, CHUNK), BF16),
            pltpu.VMEM((HL * T, DEPTH), BF16),
            pltpu.VMEM((2, 2, HL * T // 4, CHUNK), F32),
            pltpu.VMEM((HL * T, DC), F32),
            pltpu.VMEM((HL * T, 128), F32),
            pltpu.VMEM((HL * T, 128), F32),
            pltpu.VMEM((T, HL * DV), BF16),
            pltpu.VMEM((NCTX, T, WIDE), BF16),
            pltpu.VMEM((NCTX, T, WIDE), BF16),
            pltpu.VMEM((T, HL * (DN + DR)), BF16),
            pltpu.VMEM((SHARE, T), BF16),
            pltpu.VMEM((SLOTS, GRID), BF16),
            pltpu.VMEM((GRID, SLOTS), BF16),
            pltpu.VMEM((4, D, FFL), BF16),
            pltpu.VMEM((4, D, FFL), BF16),
            pltpu.VMEM((4, FFL, D), BF16),
            pltpu.VMEM((GRID, WIDE), BF16),
            pltpu.VMEM((GRID, WIDE), BF16),
            pltpu.VMEM((NCTX, 4, ROWS, WIDE), BF16),
            pltpu.VMEM((NCTX, 4, ROWS, WIDE), BF16),
            pltpu.VMEM((8, 4, ROWS, WIDE), BF16),
            pltpu.VMEM((SLOTS, WIDE), BF16),
            pltpu.VMEM((GRID, WIDE), BF16),
            pltpu.VMEM((GRID, WIDE), BF16),
            dma((11,)),
            dma((6, 32)),
            dma((6, 32)),
            dma((2, 8)),
            dma((2, 8)),
            dma((NCTX,)),
            dma((NCTX,)),
            dma((NEXP,)),
            dma((NEXP,)),
            dma((4, 8)),
            dma((4, 8)),
            dma((4, 10)),
            dma((4, 10)),
            dma((NEXP,)),
            dma((NEXP,)),
        ],
        compiler_params=pltpu.CompilerParams(
            collective_id=0, has_side_effects=True, vmem_limit_bytes=54 * 1024 * 1024
        ),
        name="layer",
    )(
        query,
        latent_cache[0].T,
        absorb_key.transpose(0, 2, 1),
        absorb_value,
        out_weight.T,
        hidden.T,
        norm_gain.reshape(D // 128, 128),
        block_mask,
        routes.T,
        route_weight.T,
        jnp.asarray(perm, BF16),
        jnp.asarray(perm.T, BF16),
        w_gate,
        w_up,
        w_down,
    )


def solution(mesh):
    in_specs = (
        P("exp", "ctx"),
        P("exp", "ctx", None),
        P("ctx", None, "exp"),
        P("ctx", "exp", None),
        P("ctx", "exp"),
        P("exp", "ctx"),
        P(),
        P(),
        P("exp", None),
        P("exp", None),
        P("exp", None, "ctx"),
        P("exp", None, "ctx"),
        P("exp", "ctx", None),
    )
    out_specs = P("exp", "ctx")
    return jax.shard_map(local, mesh=mesh, in_specs=in_specs, out_specs=out_specs, check_vma=False)
```

```python
import functools
import math

import jax
import jax.numpy as jnp
import numpy as np
from jax import lax
from jax.experimental import pallas as pl
from jax.experimental.pallas import tpu as pltpu
from jax.sharding import PartitionSpec as P

D = 3584
HL = 8
DN = 128
DR = 64
DC = 512
DV = 128
TOPK = 2
BLK = 128
SHARE = 448
WIDE = 512
T = 128
NCTX = 8
NEXP = 32
CHUNK = 512
SLOTS = 384
GRID = 512
FFL = 128
MESH = pl.DeviceIdType.MESH
F32 = jnp.float32
BF16 = jnp.bfloat16
NT = (((1,), (1,)), ((), ()))
NN = (((1,), (0,)), ((), ()))
NEG = -1e38
WO = 112
ROWS = 96
MASKED = DC + DR
CAUSAL = MASKED + 16
DEPTH = CAUSAL + T
HALF_LAT = (DC + DR) // 2
PIECE_ROWS = {1: (0, 32), 2: (32, 32), 4: (64, 48), 5: (0, WO)}
LAST_PIECE = 4

PLAN = (
    ("first", 0), ("latents", 0), ("latents", 1), ("first", 1), ("first", 2), ("prepare",), ("ring", 0, 1, 0),
    ("partner", 0), ("first", 4), ("ring", 0, 2, 0), ("ring", 0, 1, 1), ("ring", 1, 1, 0), ("first", 3),
    ("halves", 0), ("spread", 0), ("ring", 0, 3, 0), ("ring", 0, 2, 1), ("ring", 2, 1, 0), ("ring", 1, 2, 0),
    ("ring", 0, 3, 1), ("ring", 3, 1, 0), ("ring", 4, 1, 0), ("halves", 1), ("ring", 2, 2, 0), ("spread", 1),
    ("ring", 1, 3, 0), ("partner", 1), ("far", 0), ("cross", 0), ("partner", 2), ("absorb",), ("partner", 3),
    ("partner", 4), ("attend", 0, 0), ("ring", 3, 2, 0), ("attend", 0, 1), ("ring", 1, 1, 1),
    ("ring", 4, 2, 0), ("attend", 0, 2), ("attend", 0, 3), ("cross", 1), ("ring", 2, 1, 1), ("attend", 1, 0),
    ("ring", 3, 1, 1), ("ring", 4, 1, 1), ("attend", 1, 1), ("ring", 1, 2, 1), ("attend", 1, 2),
    ("ring", 2, 3, 0), ("attend", 1, 3), ("ring", 2, 2, 1), ("attend", 2, 0), ("ring", 3, 2, 1),
    ("ring", 3, 3, 0), ("attend", 2, 1), ("ring", 4, 2, 1), ("attend", 2, 2), ("ring", 4, 3, 0),
    ("attend", 2, 3), ("attend", 3, 0), ("ring", 1, 3, 1), ("ring", 2, 3, 1), ("ring", 3, 3, 1),
    ("attend", 3, 1), ("attend", 3, 2), ("ring", 4, 3, 1), ("attend", 3, 3), ("far", 1), ("far", 2),
    ("far", 3), ("far", 4), ("values",), ("project", 0), ("project", 1), ("project", -1), ("project", 2),
    ("project", -2), ("project", 3), ("project", -3), ("project", 4),
)


def dot(a, b, dims=NN):
    return lax.dot_general(a, b, dims, preferred_element_type=F32)


def remote(src, dst, send, recv, **where):
    return pltpu.make_async_remote_copy(
        src_ref=src, dst_ref=dst, send_sem=send, recv_sem=recv, device_id=where, device_id_type=MESH
    )


def place():
    c, e = lax.axis_index("ctx"), lax.axis_index("exp")
    x, y = c // 2, c % 2
    return c, e, x, y


class Around:
    def __init__(self, x, y):
        self.x, self.y = x, y

    def at(self, dx, flip):
        yy = 1 - self.y if flip else self.y
        return ((self.x + dx + 4) % 4) * 2 + yy


class Gather:
    GROUP = (0, 1, 1, 3, 4, 2, 2, 4)
    BLOCKS = (1, 2, 1, 1, 2)

    def __init__(self, view, rows, send, recv, around):
        self.view, self.rows, self.send, self.recv, self.a = view, rows, send, recv, around
        self.to = {"y": around.at(0, True), "r": around.at(1, False), "l": around.at(-1, False)}

    def op(self, i):
        a, half = self.a, self.rows // 2
        table = [
            ((0, False), (0, True), "y", 0, self.rows),
            ((0, False), (-1, False), "r", 0, self.rows),
            ((0, False), (1, False), "l", 0, self.rows),
            ((0, True), (-1, True), "r", 0, self.rows),
            ((0, True), (1, True), "l", 0, self.rows),
            ((-1, False), (2, False), "r", 0, half),
            ((1, False), (2, False), "l", half, half),
            ((2, False), (2, True), "y", 0, self.rows),
        ]
        src, got, to, first, rows = table[i]
        return a.at(*src), a.at(*got), self.to[to], first, rows

    def start(self, i, src=None):
        block, _, to, first, rows = self.op(i)
        here = self.view(block, first, rows)
        group = self.GROUP[i]
        remote(here if src is None else src, here, self.send, self.recv.at[group], ctx=to).start()

    def arrived(self, group):
        blocks = self.BLOCKS[group]
        here = self.view(pl.ds(0, blocks), 0, self.rows)
        remote(here, here, self.send, self.recv.at[group], ctx=self.to["y"]).wait_recv()

    def first(self):
        for i in range(3):
            self.start(i)

    def spread(self):
        self.arrived(0)
        self.start(3)
        self.start(4)

    def halves(self):
        self.arrived(1)
        self.start(5)
        self.start(6)

    def cross(self):
        self.arrived(2)
        self.start(7)


def layer_kernel(
    q_ref,
    lat_ref,
    ak_ref,
    av_ref,
    wo_ref,
    hid_ref,
    gain_hbm,
    mask_hbm,
    routes_hbm,
    weight_hbm,
    perm_ref,
    unperm_ref,
    wg_hbm,
    wu_hbm,
    wd_hbm,
    out_ref,
    gak,
    gav,
    gwo,
    latb,
    qlat,
    sbuf,
    acc,
    mmax,
    lsum,
    attn,
    parts,
    got,
    qb,
    hidb,
    gain_ref,
    mask_ref,
    routes_ref,
    weight_ref,
    perm,
    unperm,
    wg,
    wu,
    wd,
    xs,
    rx,
    xa,
    pd,
    tb,
    fin,
    ys,
    back,
    own_sem,
    w_send,
    w_recv,
    sib_recv,
    l_send,
    l_recv,
    r_send,
    r_recv,
    a_sems,
    g_send,
    g_recv,
    s_send,
    s_recv,
    b_sems,
    *,
    scale,
):
    c, e, x, y = place()
    z, h, k = e // 4, (e // 2) % 2, e % 2
    around = Around(x, y)

    def eid(zz, hh, kk):
        return ((zz + 16) % 8) * 4 + hh * 2 + kk

    up, down = eid(z + 1, h, k), eid(z - 1, h, k)
    partner, sibling = eid(z, 1 - h, k), eid(z, h, 1 - k)

    local_copies = [
        pltpu.make_async_copy(src, dst, own_sem.at[i])
        for i, (src, dst) in enumerate(
            (
                (ak_ref, gak.at[e]),
                (lat_ref, latb.at[c, pl.ds(0, MASKED)]),
                (av_ref, gav.at[e]),
                (wo_ref, gwo.at[e]),
                (wg_hbm, wg),
                (wu_hbm, wu),
                (wd_hbm, wd),
                (q_ref, qb),
                (hid_ref, hidb),
                (perm_ref, perm),
                (unperm_ref, unperm),
                (mask_hbm, mask_ref),
                (gain_hbm, gain_ref),
                (routes_hbm, routes_ref),
                (weight_hbm, weight_ref),
            )
        )
    ]
    early = local_copies[:4] + [local_copies[7]]
    mask_copy = local_copies[11]
    late = local_copies[4:7] + local_copies[8:11] + local_copies[12:]

    barrier = pltpu.get_barrier_semaphore()

    def hello(i, carry):
        pl.semaphore_signal(
            barrier, inc=1, device_id={"exp": (e + i) % NEXP}, device_id_type=MESH
        )
        return carry

    lax.fori_loop(1, NEXP, hello, 0)
    for i in range(1, NCTX):
        pl.semaphore_signal(
            barrier, inc=1, device_id={"ctx": (c + i) % NCTX}, device_id_type=MESH
        )
    for copy in early + [mask_copy]:
        copy.start()
    pl.semaphore_wait(barrier, NEXP - 1 + NCTX - 1)


    def piece(p, block):
        if p == 0:
            return gak.at[block]
        if p == 3:
            return gav.at[block]
        return gwo.at[block, pl.ds(*PIECE_ROWS[p])]

    def own_piece(p):
        if p == 0:
            return ak_ref
        if p == 3:
            return av_ref
        return wo_ref.at[pl.ds(*PIECE_ROWS[p])]

    def slot(off, flip, other=False):
        return eid(z + off, 1 - h if flip else h, 1 - k if other else k)

    def group_of(p):
        return {0: 0, 3: 1}.get(p, 2)

    def wcopy(p, ref, sem, to, src=None):
        return remote(ref if src is None else src, ref, w_send.at[group_of(p)], sem, exp=to)

    def ring_sem(p, off, flip):
        return w_recv.at[p, 7 if off == 4 else 1 + (off - 1) * 2 + int(flip)]

    def sibling_sem(p, off):
        return sib_recv.at[off % 8 + 2] if p == 5 else sib_recv.at[group_of(p)]

    def send_on(p, off, flip, sign, own=False):
        here = piece(p, slot(-sign * off, flip))
        src = own_piece(p) if own else None
        wcopy(p, here, ring_sem(p, off + 1, flip), up if sign > 0 else down, src).start()

    def send_sibling(p, off, flip, own=False):
        if p == LAST_PIECE:
            p = 5
        if p in (0, 3, 5):
            here = piece(p, slot(off, flip))
            wcopy(p, here, sibling_sem(p, off), sibling, own_piece(p) if own else None).start()

    def pieces(p, count):
        if p == 0:
            return gak.at[pl.ds(0, count)]
        if p == 3:
            return gav.at[pl.ds(0, count)]
        return gwo.at[pl.ds(0, count), pl.ds(*PIECE_ROWS[p])]

    def weights_first(p):
        for sign in (1, -1):
            send_on(p, 0, False, sign, True)
        wcopy(p, piece(p, e), w_recv.at[p, 0], partner, own_piece(p)).start()
        send_sibling(p, 0, False, True)

    def weights_partner(p):
        wcopy(p, pieces(p, 1), w_recv.at[p, 0], partner).wait_recv()
        for sign in (1, -1):
            send_on(p, 0, True, sign)
        send_sibling(p, 0, True)

    def weights_ring(p, off, flip):
        wcopy(p, pieces(p, 2), ring_sem(p, off, flip), partner).wait_recv()
        for sign in (1, -1):
            if off < 3 or flip == (sign < 0):
                send_on(p, off, flip, sign)
            send_sibling(p, -sign * off, flip)

    def weights_far(p):
        wcopy(p, pieces(p, 2), ring_sem(p, 4, False), partner).wait_recv()
        for flip in (False, True):
            send_sibling(p, 4, flip)

    def weights_sibling(p, off, count):
        wcopy(p, pieces(p, count), sibling_sem(p, off), sibling).wait_recv()

    def latent_view(base):
        return lambda block, first, rows: latb.at[block, pl.ds(base + first, rows)]

    lats = [
        Gather(latent_view(i * HALF_LAT), HALF_LAT, l_send.at[0], l_recv.at[i], around)
        for i in range(2)
    ]

    def latents_first(i):
        for op in range(3):
            lats[i].start(op, lat_ref.at[pl.ds(i * HALF_LAT, HALF_LAT)])

    def prepare():
        for copy in late:
            copy.start()
        mask_copy.wait()
        blocks = NCTX * CHUNK // BLK
        last = mask_ref[blocks - 1 : blocks, :].astype(F32)
        at = lax.broadcasted_iota(jnp.int32, (1, blocks), 1)
        top = lax.broadcasted_iota(jnp.int32, (16, BLK), 0) == 0

        def fill(i, carry):
            for b in range(CHUNK // BLK):
                cols = slice(b * BLK, (b + 1) * BLK)
                here = at == i * (CHUNK // BLK) + b
                is_open = jnp.sum(jnp.where(here, last, 0.0), axis=1, keepdims=True)
                taken = jnp.where(top, NEG, 0.0) * (1.0 - is_open)
                latb[i, MASKED:CAUSAL, cols] = taken.astype(BF16)
            latb[i, CAUSAL:DEPTH, :] = jnp.zeros((T, CHUNK), BF16)
            return carry

        lax.fori_loop(0, NCTX, fill, 0)
        latb[NCTX - 1, CAUSAL:DEPTH, CHUNK - T : CHUNK] = jnp.where(lane > sub, NEG, 0.0).astype(BF16)
        ones = jnp.where(lane[:, 0:16] == 0, 1.0, 0.0).astype(BF16)
        for head in range(HL):
            qlat[head * T : (head + 1) * T, MASKED:CAUSAL] = ones
            qlat[head * T : (head + 1) * T, CAUSAL:DEPTH] = eye

    sub = lax.broadcasted_iota(jnp.int32, (T, T), 0)
    lane = lax.broadcasted_iota(jnp.int32, (T, T), 1)
    eye = jnp.where(sub == lane, 1.0, 0.0).astype(BF16)

    def column(row):
        return jnp.sum(jnp.where(sub == lane, row, 0.0), axis=1, keepdims=True)

    def places():
        earlier = jnp.where(sub < lane, 1.0, 0.0).astype(BF16)
        expert_of_row = sub.astype(F32)
        routes = [routes_ref[i : i + 1, :].astype(F32) for i in range(TOPK)]
        named = [jnp.where(expert_of_row == r, 1.0, 0.0) for r in routes]
        before = dot((named[0] + named[1]).astype(BF16), earlier)
        return [
            r * 4 + jnp.sum(before * n, axis=0, keepdims=True)
            for r, n in zip(routes, named, strict=True)
        ]

    def absorb():
        weights_sibling(0, 0, 16)
        for copy in early:
            copy.wait()

        def body(i, carry):
            pair_q = qb[:, pl.ds(pl.multiple_of(i * 384, 384), 384)]
            for j in range(2):
                at = j * (DN + DR)
                rows = pl.ds(pl.multiple_of(i * 2 * T + j * T, T), T)
                weight = gak[:, pl.ds(i * 2 + j, 1)].reshape(DC, DN)
                qlat[rows, 0:DC] = (dot(pair_q[:, at : at + DN], weight, NT) * factor).astype(BF16)
                rope = pair_q[:, at + DN : at + DN + DR].astype(F32) * factor
                qlat[rows, DC : DC + DR] = rope.astype(BF16)
            return carry

        lax.fori_loop(0, HL // 2, body, 0)

    factor = scale * math.log2(math.e)
    groups = [
        [around.at(0, False), around.at(0, True)],
        [around.at(-1, False), around.at(1, False)],
        [around.at(2, False), around.at(-1, True)],
        [around.at(1, True), around.at(2, True)],
    ]
    step_rows = HL * T // 4

    def score(g, q):
        rows = pl.ds(q * step_rows, step_rows)
        for i, b in enumerate(groups[g]):
            sbuf[q % 2, i] = dot(qlat[rows, :], latb[b])

    def attend(g, q):
        if q == 0:
            for piece_of in lats:
                if g == 2:
                    piece_of.arrived(3)
                if g == 3:
                    piece_of.arrived(4)
            score(g, 0)
        if q < 3:
            score(g, q + 1)
        rows = pl.ds(q * step_rows, step_rows)
        scores = [sbuf[q % 2, i] for i in range(2)]
        top = jnp.max(jnp.maximum(*scores), axis=1, keepdims=True)
        if g > 0:
            old = mmax[rows, 0:1]
            top = jnp.maximum(old, top)
        probs = [jnp.exp2(s - top) for s in scores]
        total = jnp.sum(probs[0] + probs[1], axis=1, keepdims=True)
        product = sum(
            dot(p.astype(BF16), latb[b, 0:DC, :], NT)
            for p, b in zip(probs, groups[g], strict=True)
        )
        if g > 0:
            shrink = jnp.exp2(old - top)
            total = total + lsum[rows, 0:1] * shrink
            product = product + acc[rows, :] * shrink
        mmax[rows, :] = jnp.broadcast_to(top, (step_rows, 128))
        lsum[rows, :] = jnp.broadcast_to(total, (step_rows, 128))
        acc[rows, :] = product

    def values():
        weights_sibling(3, 0, 16)

        def body(head, carry):
            cols = pl.ds(pl.multiple_of(head * DV, DV), DV)
            rows = pl.ds(pl.multiple_of(head * T, T), T)
            weight = gav[:, pl.ds(head, 1)].reshape(DC, DV)
            latent_out = (acc[rows, :] * (1.0 / lsum[rows, 0:1])).astype(BF16)
            attn[:, cols] = dot(latent_out, weight).astype(BF16)
            return carry

        lax.fori_loop(0, HL, body, 0)


    def rcopy(dest, source):
        return remote(parts.at[dest], got.at[source], r_send.at[0], r_recv.at[0], ctx=dest)

    def project(off):
        weights_sibling(5, off, 2)
        dest = (z + off + 8) % 8
        weight = gwo[pl.ds(dest * 4, 4)].reshape(SHARE, HL * DV)
        partial = dot(attn[...], weight, NT)
        parts[dest, :, 0:SHARE] = partial.astype(BF16)
        parts[dest, :, SHARE:WIDE] = jnp.zeros((T, WIDE - SHARE), BF16)

        @pl.when(dest != c)
        def _():
            rcopy(dest, c).start()

        @pl.when(dest == c)
        def _():
            got[c] = parts[dest]

    acts = {
        "first": weights_first,
        "partner": weights_partner,
        "ring": weights_ring,
        "far": weights_far,
        "latents": latents_first,
        "spread": lambda i: lats[i].spread(),
        "halves": lambda i: lats[i].halves(),
        "cross": lambda i: lats[i].cross(),
        "prepare": prepare,
        "absorb": absorb,
        "attend": attend,
        "values": values,
        "project": project,
    }
    for act, *how in PLAN:
        acts[act](*how)

    here = got.at[pl.ds(0, NCTX - 1)]
    remote(here, here, r_send.at[0], r_recv.at[0], ctx=around.at(0, True)).wait_recv()
    for copy in late:
        copy.wait()
    place_rows = places()
    place_cols = [column(r) for r in place_rows]
    resid = dot(eye, hidb[...], NT)
    for i in range(NCTX):
        resid = resid + got[i, :, 0:SHARE].astype(F32)

    squares = jnp.sum(resid * resid, axis=1, keepdims=True)
    high = squares.astype(BF16).astype(F32)
    low = squares - high
    beside = lax.broadcasted_iota(jnp.int32, (T, WIDE - SHARE), 1)
    tail = jnp.where(beside == 0, high, jnp.where(beside == 1, low, 0.0))
    gains = jnp.concatenate([gain_ref[pl.ds(x * 7 + i, 1), :] for i in range(7)], axis=1)
    gain = jnp.where(y == 0, gains[:, 0:SHARE], gains[:, SHARE:])
    scaled = jnp.concatenate([resid * gain, tail], axis=1).astype(BF16)
    where = lax.broadcasted_iota(jnp.int32, (GRID, T), 0).astype(F32)
    chosen = (where == place_rows[0]) | (where == place_rows[1])
    xs[...] = dot(jnp.where(chosen, 1.0, 0.0).astype(BF16), scaled).astype(BF16)

    def rows16(i):
        return pl.ds(pl.multiple_of(i * 16, 16), 16)

    def exchange(src, dst, sems):
        def go(i, carry):
            to = (e + i) % NEXP
            here, there = src.at[rows16(to)], dst.at[rows16(e)]
            remote(here, there, sems.at[0], sems.at[1], exp=to).start()
            return carry

        lax.fori_loop(1, NEXP, go, 0)
        dst[rows16(e), :] = src[rows16(e), :]
        everything = pl.ds(0, (NEXP - 1) * 16)
        all_sent = remote(src.at[everything], dst.at[everything], sems.at[0], sems.at[1], exp=sibling)
        all_sent.wait_recv()
        return all_sent

    a_left = exchange(xs, rx, a_sems)
    for j in range(4):
        xa[c, j] = dot(perm[j * ROWS : (j + 1) * ROWS, :], rx[...]).astype(BF16)

    def rows_view(j):
        return lambda block, first, rows: xa.at[block, j, pl.ds(first, rows)]

    gathers = [Gather(rows_view(j), ROWS, g_send.at[0], g_recv.at[j], around) for j in range(4)]
    for g in gathers:
        g.first()

    lanes = lax.broadcasted_iota(jnp.int32, (ROWS, 128), 1)

    def expert(j):
        gathers[j].arrived(3)
        gathers[j].arrived(4)

        def feed(block, carry):
            g, u, t = carry
            rows_c = pl.ds(pl.multiple_of(block * SHARE, SHARE), SHARE)
            lhs = xa[block, j, :, 0:SHARE]
            g = g + dot(lhs, wg[j, rows_c, :])
            u = u + dot(lhs, wu[j, rows_c, :])
            return g, u, t + xa[block, j, :, 384:WIDE].astype(F32)

        zero = jnp.zeros((ROWS, FFL), F32)
        g, u, t = lax.fori_loop(0, NCTX, feed, (zero, zero, zero))
        kept = jnp.where((lanes == 64) | (lanes == 65), t, 0.0)
        inv = lax.rsqrt(jnp.sum(kept, axis=1, keepdims=True) / D + 1e-06)
        g, u = g * inv, u * inv
        act = (g / (1.0 + jnp.exp(-g)) * u).astype(BF16)

        def produce(xx, carry):
            cols = pl.ds(pl.multiple_of(xx * 2 * SHARE, 2 * SHARE), 2 * SHARE)
            both = dot(act, wd[j, :, cols]).astype(BF16)
            blank = jnp.zeros((ROWS, WIDE - SHARE), BF16)
            pd[xx * 2, j, :, 0:SHARE] = both[:, 0:SHARE]
            pd[xx * 2 + 1, j, :, 0:SHARE] = both[:, SHARE:]
            pd[xx * 2, j, :, SHARE:WIDE] = blank
            pd[xx * 2 + 1, j, :, SHARE:WIDE] = blank
            return carry

        lax.fori_loop(0, NCTX // 2, produce, 0)
        for i in (0, 1, 2, 6, 7):
            scopy(j, i).start()

    half = ROWS // 2
    lo, hi, whole = pl.ds(0, half), pl.ds(half, half), pl.ds(0, ROWS)
    yp, xr, xl = around.at(0, True), around.at(1, False), around.at(-1, False)
    sends = [
        (around.at(2, True), whole, 0, yp),
        (around.at(1, True), whole, 1, xr),
        (around.at(-1, True), whole, 2, xl),
        (around.at(2, False), lo, 3, xr),
        (around.at(2, False), hi, 4, xl),
        (around.at(0, True), whole, 5, yp),
        (around.at(1, False), hi, 6, xr),
        (around.at(-1, False), lo, 7, xl),
        (around.at(1, False), lo, 6, xr),
        (around.at(-1, False), hi, 7, xl),
    ]

    groups_of = (0, 1, 1, 2, 2, 3, 3, 3, 3, 3)
    whole_blocks = (1, 2, 1, 3)

    def scopy(j, i):
        block, rows, land, to = sends[i]
        here, there = pd.at[block, j, rows], tb.at[land, j, rows]
        return remote(here, there, s_send.at[0], s_recv.at[j, groups_of[i]], ctx=to)

    def sgot(j, group):
        here = tb.at[pl.ds(0, whole_blocks[group]), j]
        remote(here, here, s_send.at[0], s_recv.at[j, group], ctx=yp).wait_recv()

    def add(j, block, rows, *lands):
        total = pd[block, j, rows, :].astype(F32)
        for land in lands:
            total = total + tb[land, j, rows, :].astype(F32)
        pd[block, j, rows, :] = total.astype(BF16)

    def reduce1(j):
        sgot(j, 0)
        add(j, around.at(2, False), whole, 0)
        scopy(j, 3).start()
        scopy(j, 4).start()
        sgot(j, 1)
        add(j, around.at(0, True), whole, 1, 2)
        scopy(j, 5).start()

    def reduce2(j):
        sgot(j, 2)
        add(j, around.at(1, False), lo, 3)
        scopy(j, 8).start()
        add(j, around.at(-1, False), hi, 4)
        scopy(j, 9).start()

    def reduce3(j):
        sgot(j, 3)
        total = pd[c, j].astype(F32)
        for land in (5, 6, 7):
            total = total + tb[land, j].astype(F32)
        fin[j * ROWS : (j + 1) * ROWS, :] = total.astype(BF16)

    gathers[0].spread()
    gathers[0].halves()
    gathers[1].spread()
    gathers[1].halves()
    gathers[0].cross()
    gathers[2].spread()
    gathers[2].halves()
    gathers[3].spread()
    gathers[3].halves()
    gathers[1].cross()
    expert(0)
    gathers[2].cross()
    gathers[3].cross()
    expert(1)
    reduce1(0)
    expert(2)
    reduce1(1)
    reduce2(0)
    expert(3)
    reduce1(2)
    reduce2(1)
    reduce3(0)
    reduce1(3)
    reduce2(2)
    reduce3(1)
    reduce2(3)
    reduce3(2)
    reduce3(3)
    ys[...] = dot(unperm[...], fin[...]).astype(BF16)

    b_left = exchange(ys, back, b_sems)
    spots = lax.broadcasted_iota(jnp.int32, (T, GRID), 1).astype(F32)
    result = resid
    for i in range(TOPK):
        picked = jnp.where(spots == place_cols[i], 1.0, 0.0).astype(BF16)
        result = result + dot(picked, back[...])[:, 0:SHARE] * column(weight_ref[i : i + 1, :])
    out_ref[...] = result.astype(BF16)

    for p, group in ((0, 0), (3, 1), (5, 2)):
        wcopy(p, pieces(p, NEXP - 1), w_recv.at[0, 0], sibling).wait_send()
    seven = pl.ds(0, NCTX - 1)
    for sent, sem in (
        (latb.at[seven, pl.ds(0, MASKED)], l_send),
        (parts.at[seven], r_send),
        (xa.at[seven], g_send),
        (pd.at[seven], s_send),
    ):
        remote(sent, sent, sem.at[0], r_recv.at[0], ctx=yp).wait_send()
    a_left.wait_send()
    b_left.wait_send()


def permutations():
    perm = np.zeros((SLOTS, GRID), np.float32)
    for j in range(4):
        for s in range(NEXP):
            for i in range(3):
                perm[j * ROWS + s * 3 + i, s * 16 + j * 4 + i] = 1.0
    return perm


VMEM = pl.BlockSpec(memory_space=pltpu.VMEM)
ANY = pl.BlockSpec(memory_space=pl.ANY)


def local(
    query,
    latent_cache,
    absorb_key,
    absorb_value,
    out_weight,
    hidden,
    norm_gain,
    block_mask,
    routes,
    route_weight,
    w_gate,
    w_up,
    w_down,
):
    perm = permutations()
    dma = pltpu.SemaphoreType.DMA
    return pl.pallas_call(
        functools.partial(layer_kernel, scale=1.0 / math.sqrt(DN + DR)),
        out_shape=jax.ShapeDtypeStruct((T, SHARE), BF16),
        in_specs=[ANY] * 15,
        out_specs=VMEM,
        scratch_shapes=[
            pltpu.VMEM((NEXP, HL, 16, DN), BF16),
            pltpu.VMEM((NEXP, HL, 16, DV), BF16),
            pltpu.VMEM((NEXP, WO, HL * DV), BF16),
            pltpu.VMEM((NCTX, DEPTH, CHUNK), BF16),
            pltpu.VMEM((HL * T, DEPTH), BF16),
            pltpu.VMEM((2, 2, HL * T // 4, CHUNK), F32),
            pltpu.VMEM((HL * T, DC), F32),
            pltpu.VMEM((HL * T, 128), F32),
            pltpu.VMEM((HL * T, 128), F32),
            pltpu.VMEM((T, HL * DV), BF16),
            pltpu.VMEM((NCTX, T, WIDE), BF16),
            pltpu.VMEM((NCTX, T, WIDE), BF16),
            pltpu.VMEM((T, HL * (DN + DR)), BF16),
            pltpu.VMEM((SHARE, T), BF16),
            pltpu.VMEM((D // 128, 128), F32),
            pltpu.VMEM((32, 32), jnp.int32),
            pltpu.VMEM((TOPK, T), jnp.int32),
            pltpu.VMEM((TOPK, T), F32),
            pltpu.VMEM((SLOTS, GRID), BF16),
            pltpu.VMEM((GRID, SLOTS), BF16),
            pltpu.VMEM((4, D, FFL), BF16),
            pltpu.VMEM((4, D, FFL), BF16),
            pltpu.VMEM((4, FFL, D), BF16),
            pltpu.VMEM((GRID, WIDE), BF16),
            pltpu.VMEM((GRID, WIDE), BF16),
            pltpu.VMEM((NCTX, 4, ROWS, WIDE), BF16),
            pltpu.VMEM((NCTX, 4, ROWS, WIDE), BF16),
            pltpu.VMEM((8, 4, ROWS, WIDE), BF16),
            pltpu.VMEM((SLOTS, WIDE), BF16),
            pltpu.VMEM((GRID, WIDE), BF16),
            pltpu.VMEM((GRID, WIDE), BF16),
            dma((15,)),
            dma((3,)),
            dma((5, 8)),
            dma((10,)),
            dma((1,)),
            dma((2, 5)),
            dma((1,)),
            dma((1,)),
            dma((2,)),
            dma((1,)),
            dma((4, 5)),
            dma((1,)),
            dma((4, 4)),
            dma((2,)),
        ],
        compiler_params=pltpu.CompilerParams(
            collective_id=0, has_side_effects=True, vmem_limit_bytes=54 * 1024 * 1024
        ),
        name="layer",
    )(
        query,
        latent_cache[0].T,
        absorb_key.transpose(0, 2, 1),
        absorb_value,
        out_weight.T,
        hidden.T,
        norm_gain.reshape(D // 128, 128),
        block_mask,
        routes.T,
        route_weight.T,
        jnp.asarray(perm, BF16),
        jnp.asarray(perm.T, BF16),
        w_gate,
        w_up,
        w_down,
    )


def solution(mesh):
    in_specs = (
        P("exp", "ctx"),
        P("exp", "ctx", None),
        P("ctx", None, "exp"),
        P("ctx", "exp", None),
        P("ctx", "exp"),
        P("exp", "ctx"),
        P(),
        P(),
        P("exp", None),
        P("exp", None),
        P("exp", None, "ctx"),
        P("exp", None, "ctx"),
        P("exp", "ctx", None),
    )
    out_specs = P("exp", "ctx")
    return jax.shard_map(local, mesh=mesh, in_specs=in_specs, out_specs=out_specs, check_vma=False)
```

```python
import functools
import math

import jax
import jax.numpy as jnp
import numpy as np
from jax import lax
from jax.experimental import pallas as pl
from jax.experimental.pallas import tpu as pltpu
from jax.sharding import PartitionSpec as P

D = 3584
HL = 8
DN = 128
DR = 64
DC = 512
DV = 128
TOPK = 2
BLK = 128
SHARE = 448
WIDE = 512
MAIN = 384
T = 128
NCTX = 8
NEXP = 32
CHUNK = 512
SLOTS = 384
GRID = 512
FFL = 128
MESH = pl.DeviceIdType.MESH
F32 = jnp.float32
BF16 = jnp.bfloat16
NT = (((1,), (1,)), ((), ()))
NN = (((1,), (0,)), ((), ()))
NEG = -1e38
WO = 112
ROWS = 96
MASKED = DC + DR
CAUSAL = MASKED + 16
DEPTH = CAUSAL + T
HALF_LAT = (DC + DR) // 2
PIECE_ROWS = {1: (0, 32), 2: (32, 32), 4: (64, 48), 5: (0, WO)}
LAST_PIECE = 4

PLAN = (
    ("first", 0), ("latents", 0), ("latents", 1), ("first", 1), ("first", 2), ("prepare",), ("ring", 0, 1, 0),
    ("partner", 0), ("first", 4), ("ring", 0, 2, 0), ("ring", 0, 1, 1), ("ring", 1, 1, 0), ("first", 3),
    ("halves", 0), ("spread", 0), ("ring", 0, 3, 0), ("ring", 0, 2, 1), ("ring", 2, 1, 0), ("ring", 1, 2, 0),
    ("ring", 0, 3, 1), ("ring", 3, 1, 0), ("ring", 4, 1, 0), ("halves", 1), ("ring", 2, 2, 0), ("spread", 1),
    ("ring", 1, 3, 0), ("partner", 1), ("far", 0), ("cross", 0), ("partner", 2), ("absorb",), ("partner", 3),
    ("partner", 4), ("attend", 0, 0), ("ring", 3, 2, 0), ("attend", 0, 1), ("ring", 1, 1, 1),
    ("ring", 4, 2, 0), ("attend", 0, 2), ("attend", 0, 3), ("cross", 1), ("ring", 2, 1, 1), ("attend", 1, 0),
    ("ring", 3, 1, 1), ("ring", 4, 1, 1), ("attend", 1, 1), ("ring", 1, 2, 1), ("attend", 1, 2),
    ("ring", 2, 3, 0), ("attend", 1, 3), ("ring", 2, 2, 1), ("attend", 2, 0), ("ring", 3, 2, 1),
    ("ring", 3, 3, 0), ("attend", 2, 1), ("ring", 4, 2, 1), ("attend", 2, 2), ("ring", 4, 3, 0),
    ("attend", 2, 3), ("attend", 3, 0), ("ring", 1, 3, 1), ("ring", 2, 3, 1), ("ring", 3, 3, 1),
    ("attend", 3, 1), ("attend", 3, 2), ("ring", 4, 3, 1), ("attend", 3, 3), ("far", 1), ("far", 2),
    ("far", 3), ("far", 4), ("values",), ("project", 0), ("project", 1), ("project", -1), ("project", 2),
    ("project", -2), ("project", 3), ("project", -3), ("project", 4),
)


def dot(a, b, dims=NN):
    return lax.dot_general(a, b, dims, preferred_element_type=F32)


def remote(src, dst, send, recv, **where):
    return pltpu.make_async_remote_copy(
        src_ref=src, dst_ref=dst, send_sem=send, recv_sem=recv, device_id=where, device_id_type=MESH
    )


def place():
    c, e = lax.axis_index("ctx"), lax.axis_index("exp")
    x, y = c // 2, c % 2
    return c, e, x, y


class Around:
    def __init__(self, x, y):
        self.x, self.y = x, y

    def at(self, dx, flip):
        yy = 1 - self.y if flip else self.y
        return ((self.x + dx + 4) % 4) * 2 + yy


class Gather:
    GROUP = (0, 1, 1, 3, 4, 2, 2, 4)
    BLOCKS = (1, 2, 1, 1, 2)

    def __init__(self, view, rows, send, recv, around):
        self.view, self.rows, self.send, self.recv, self.a = view, rows, send, recv, around
        self.to = {"y": around.at(0, True), "r": around.at(1, False), "l": around.at(-1, False)}

    def op(self, i):
        a, half = self.a, self.rows // 2
        table = [
            ((0, False), (0, True), "y", 0, self.rows),
            ((0, False), (-1, False), "r", 0, self.rows),
            ((0, False), (1, False), "l", 0, self.rows),
            ((0, True), (-1, True), "r", 0, self.rows),
            ((0, True), (1, True), "l", 0, self.rows),
            ((-1, False), (2, False), "r", 0, half),
            ((1, False), (2, False), "l", half, half),
            ((2, False), (2, True), "y", 0, self.rows),
        ]
        src, got, to, first, rows = table[i]
        return a.at(*src), a.at(*got), self.to[to], first, rows

    def start(self, i, src=None):
        block, _, to, first, rows = self.op(i)
        here = self.view(block, first, rows)
        group = self.GROUP[i]
        remote(here if src is None else src, here, self.send, self.recv.at[group], ctx=to).start()

    def arrived(self, group):
        blocks = self.BLOCKS[group]
        here = self.view(pl.ds(0, blocks), 0, self.rows)
        remote(here, here, self.send, self.recv.at[group], ctx=self.to["y"]).wait_recv()

    def first(self):
        for i in range(3):
            self.start(i)

    def spread(self):
        self.arrived(0)
        self.start(3)
        self.start(4)

    def halves(self):
        self.arrived(1)
        self.start(5)
        self.start(6)

    def cross(self):
        self.arrived(2)
        self.start(7)


def layer_kernel(
    q_ref,
    lat_ref,
    ak_ref,
    av_ref,
    wo_ref,
    hid_ref,
    gain_hbm,
    mask_hbm,
    routes_hbm,
    weight_hbm,
    perm_ref,
    unperm_ref,
    wg_hbm,
    wu_hbm,
    wd_hbm,
    out_ref,
    gak,
    gav,
    gwo,
    latb,
    qlat,
    sbuf,
    acc,
    mmax,
    lsum,
    attn,
    parts,
    got,
    qb,
    hidb,
    gain_ref,
    mask_ref,
    routes_ref,
    weight_ref,
    perm,
    unperm,
    wg,
    wu,
    wd,
    xs,
    rx,
    xa,
    pd,
    tb,
    fin,
    ys,
    back,
    own_sem,
    w_send,
    w_recv,
    sib_recv,
    l_send,
    l_recv,
    r_send,
    r_recv,
    a_sems,
    g_send,
    g_recv,
    s_send,
    s_recv,
    b_sems,
    *,
    scale,
):
    c, e, x, y = place()
    z, h, k = e // 4, (e // 2) % 2, e % 2
    around = Around(x, y)

    def eid(zz, hh, kk):
        return ((zz + 16) % 8) * 4 + hh * 2 + kk

    up, down = eid(z + 1, h, k), eid(z - 1, h, k)
    partner, sibling = eid(z, 1 - h, k), eid(z, h, 1 - k)

    local_copies = [
        pltpu.make_async_copy(src, dst, own_sem.at[i])
        for i, (src, dst) in enumerate(
            (
                (ak_ref, gak.at[e]),
                (lat_ref, latb.at[c, pl.ds(0, MASKED)]),
                (av_ref, gav.at[e]),
                (wo_ref, gwo.at[e]),
                (wg_hbm, wg),
                (wu_hbm, wu),
                (wd_hbm, wd),
                (q_ref, qb),
                (hid_ref, hidb),
                (perm_ref, perm),
                (unperm_ref, unperm),
                (mask_hbm, mask_ref),
                (gain_hbm, gain_ref),
                (routes_hbm, routes_ref),
                (weight_hbm, weight_ref),
            )
        )
    ]
    early = local_copies[:4] + [local_copies[7]]
    mask_copy = local_copies[11]
    late = local_copies[4:7] + local_copies[8:11] + local_copies[12:]

    barrier = pltpu.get_barrier_semaphore()

    peers = [{"exp": d} for d in (up, down, partner, sibling)]
    peers += [{"ctx": (c + i) % NCTX} for i in range(1, NCTX)]
    for where in peers:
        pl.semaphore_signal(barrier, inc=1, device_id=where, device_id_type=MESH)
    for copy in early + [mask_copy]:
        copy.start()
    pl.semaphore_wait(barrier, len(peers))


    def piece(p, block):
        if p == 0:
            return gak.at[block]
        if p == 3:
            return gav.at[block]
        return gwo.at[block, pl.ds(*PIECE_ROWS[p])]

    def own_piece(p):
        if p == 0:
            return ak_ref
        if p == 3:
            return av_ref
        return wo_ref.at[pl.ds(*PIECE_ROWS[p])]

    def slot(off, flip, other=False):
        return eid(z + off, 1 - h if flip else h, 1 - k if other else k)

    def group_of(p):
        return {0: 0, 3: 1}.get(p, 2)

    def wcopy(p, ref, sem, to, src=None):
        return remote(ref if src is None else src, ref, w_send.at[group_of(p)], sem, exp=to)

    def ring_sem(p, off, flip):
        return w_recv.at[p, 7 if off == 4 else 1 + (off - 1) * 2 + int(flip)]

    def sibling_sem(p, off):
        return sib_recv.at[off % 8 + 2] if p == 5 else sib_recv.at[group_of(p)]

    def send_on(p, off, flip, sign, own=False):
        here = piece(p, slot(-sign * off, flip))
        src = own_piece(p) if own else None
        wcopy(p, here, ring_sem(p, off + 1, flip), up if sign > 0 else down, src).start()

    def send_sibling(p, off, flip, own=False):
        if p == LAST_PIECE:
            p = 5
        if p in (0, 3, 5):
            here = piece(p, slot(off, flip))
            wcopy(p, here, sibling_sem(p, off), sibling, own_piece(p) if own else None).start()

    def pieces(p, count):
        if p == 0:
            return gak.at[pl.ds(0, count)]
        if p == 3:
            return gav.at[pl.ds(0, count)]
        return gwo.at[pl.ds(0, count), pl.ds(*PIECE_ROWS[p])]

    def weights_first(p):
        for sign in (1, -1):
            send_on(p, 0, False, sign, True)
        wcopy(p, piece(p, e), w_recv.at[p, 0], partner, own_piece(p)).start()
        send_sibling(p, 0, False, True)

    def weights_partner(p):
        wcopy(p, pieces(p, 1), w_recv.at[p, 0], partner).wait_recv()
        for sign in (1, -1):
            send_on(p, 0, True, sign)
        send_sibling(p, 0, True)

    def weights_ring(p, off, flip):
        wcopy(p, pieces(p, 2), ring_sem(p, off, flip), partner).wait_recv()
        for sign in (1, -1):
            if off < 3 or flip == (sign < 0):
                send_on(p, off, flip, sign)
            send_sibling(p, -sign * off, flip)

    def weights_far(p):
        wcopy(p, pieces(p, 2), ring_sem(p, 4, False), partner).wait_recv()
        for flip in (False, True):
            send_sibling(p, 4, flip)

    def weights_sibling(p, off, count):
        wcopy(p, pieces(p, count), sibling_sem(p, off), sibling).wait_recv()

    def latent_view(base):
        return lambda block, first, rows: latb.at[block, pl.ds(base + first, rows)]

    lats = [
        Gather(latent_view(i * HALF_LAT), HALF_LAT, l_send.at[0], l_recv.at[i], around)
        for i in range(2)
    ]

    def latents_first(i):
        for op in range(3):
            lats[i].start(op, lat_ref.at[pl.ds(i * HALF_LAT, HALF_LAT)])

    def prepare():
        for copy in late:
            copy.start()
        mask_copy.wait()
        blocks = NCTX * CHUNK // BLK
        last = mask_ref[blocks - 1 : blocks, :].astype(F32)
        at = lax.broadcasted_iota(jnp.int32, (1, blocks), 1)
        top = lax.broadcasted_iota(jnp.int32, (16, BLK), 0) == 0

        def fill(i, carry):
            for b in range(CHUNK // BLK):
                cols = slice(b * BLK, (b + 1) * BLK)
                here = at == i * (CHUNK // BLK) + b
                is_open = jnp.sum(jnp.where(here, last, 0.0), axis=1, keepdims=True)
                taken = jnp.where(top, NEG, 0.0) * (1.0 - is_open)
                latb[i, MASKED:CAUSAL, cols] = taken.astype(BF16)
            latb[i, CAUSAL:DEPTH, :] = jnp.zeros((T, CHUNK), BF16)
            return carry

        lax.fori_loop(0, NCTX, fill, 0)
        latb[NCTX - 1, CAUSAL:DEPTH, CHUNK - T : CHUNK] = jnp.where(lane > sub, NEG, 0.0).astype(BF16)
        ones = jnp.where(lane[:, 0:16] == 0, 1.0, 0.0).astype(BF16)
        for head in range(HL):
            qlat[head * T : (head + 1) * T, MASKED:CAUSAL] = ones
            qlat[head * T : (head + 1) * T, CAUSAL:DEPTH] = eye

    sub = lax.broadcasted_iota(jnp.int32, (T, T), 0)
    lane = lax.broadcasted_iota(jnp.int32, (T, T), 1)
    eye = jnp.where(sub == lane, 1.0, 0.0).astype(BF16)

    def column(row):
        return jnp.sum(jnp.where(sub == lane, row, 0.0), axis=1, keepdims=True)

    def places():
        earlier = jnp.where(sub < lane, 1.0, 0.0).astype(BF16)
        expert_of_row = sub.astype(F32)
        routes = [routes_ref[i : i + 1, :].astype(F32) for i in range(TOPK)]
        named = [jnp.where(expert_of_row == r, 1.0, 0.0) for r in routes]
        before = dot((named[0] + named[1]).astype(BF16), earlier)
        return [
            r * 4 + jnp.sum(before * n, axis=0, keepdims=True)
            for r, n in zip(routes, named, strict=True)
        ]

    def absorb():
        weights_sibling(0, 0, 16)
        for copy in early:
            copy.wait()

        def body(i, carry):
            pair_q = qb[:, pl.ds(pl.multiple_of(i * 384, 384), 384)]
            for j in range(2):
                at = j * (DN + DR)
                rows = pl.ds(pl.multiple_of(i * 2 * T + j * T, T), T)
                weight = gak[:, pl.ds(i * 2 + j, 1)].reshape(DC, DN)
                qlat[rows, 0:DC] = (dot(pair_q[:, at : at + DN], weight, NT) * factor).astype(BF16)
                rope = pair_q[:, at + DN : at + DN + DR].astype(F32) * factor
                qlat[rows, DC : DC + DR] = rope.astype(BF16)
            return carry

        lax.fori_loop(0, HL // 2, body, 0)

    factor = scale * math.log2(math.e)
    groups = [
        [around.at(0, False), around.at(0, True)],
        [around.at(-1, False), around.at(1, False)],
        [around.at(2, False), around.at(-1, True)],
        [around.at(1, True), around.at(2, True)],
    ]
    step_rows = HL * T // 4

    def score(g, q):
        rows = pl.ds(q * step_rows, step_rows)
        for i, b in enumerate(groups[g]):
            sbuf[q % 2, i] = dot(qlat[rows, :], latb[b])

    def attend(g, q):
        if q == 0:
            for piece_of in lats:
                if g == 2:
                    piece_of.arrived(3)
                if g == 3:
                    piece_of.arrived(4)
            score(g, 0)
        if q < 3:
            score(g, q + 1)
        rows = pl.ds(q * step_rows, step_rows)
        scores = [sbuf[q % 2, i] for i in range(2)]
        top = jnp.max(jnp.maximum(*scores), axis=1, keepdims=True)
        if g > 0:
            old = mmax[rows, 0:1]
            top = jnp.maximum(old, top)
        probs = [jnp.exp2(s - top) for s in scores]
        total = jnp.sum(probs[0] + probs[1], axis=1, keepdims=True)
        product = sum(
            dot(p.astype(BF16), latb[b, 0:DC, :], NT)
            for p, b in zip(probs, groups[g], strict=True)
        )
        if g > 0:
            shrink = jnp.exp2(old - top)
            total = total + lsum[rows, 0:1] * shrink
            product = product + acc[rows, :] * shrink
        mmax[rows, :] = jnp.broadcast_to(top, (step_rows, 128))
        lsum[rows, :] = jnp.broadcast_to(total, (step_rows, 128))
        acc[rows, :] = product

    def values():
        weights_sibling(3, 0, 16)

        def body(head, carry):
            cols = pl.ds(pl.multiple_of(head * DV, DV), DV)
            rows = pl.ds(pl.multiple_of(head * T, T), T)
            weight = gav[:, pl.ds(head, 1)].reshape(DC, DV)
            latent_out = (acc[rows, :] * (1.0 / lsum[rows, 0:1])).astype(BF16)
            attn[:, cols] = dot(latent_out, weight).astype(BF16)
            return carry

        lax.fori_loop(0, HL, body, 0)


    def rcopy(dest, source):
        return remote(parts.at[dest], got.at[source], r_send.at[0], r_recv.at[0], ctx=dest)

    def project(off):
        weights_sibling(5, off, 2)
        dest = (z + off + 8) % 8
        weight = gwo[pl.ds(dest * 4, 4)].reshape(SHARE, HL * DV)
        partial = dot(attn[...], weight, NT)
        parts[dest, :, 0:SHARE] = partial.astype(BF16)
        parts[dest, :, SHARE:WIDE] = jnp.zeros((T, WIDE - SHARE), BF16)

        @pl.when(dest != c)
        def _():
            rcopy(dest, c).start()

        @pl.when(dest == c)
        def _():
            got[c] = parts[dest]

    acts = {
        "first": weights_first,
        "partner": weights_partner,
        "ring": weights_ring,
        "far": weights_far,
        "latents": latents_first,
        "spread": lambda i: lats[i].spread(),
        "halves": lambda i: lats[i].halves(),
        "cross": lambda i: lats[i].cross(),
        "prepare": prepare,
        "absorb": absorb,
        "attend": attend,
        "values": values,
        "project": project,
    }
    for act, *how in PLAN:
        acts[act](*how)

    here = got.at[pl.ds(0, NCTX - 1)]
    remote(here, here, r_send.at[0], r_recv.at[0], ctx=around.at(0, True)).wait_recv()
    for copy in late:
        copy.wait()
    place_rows = places()
    place_cols = [column(r) for r in place_rows]
    resid = dot(eye, hidb[...], NT)
    for i in range(NCTX):
        resid = resid + got[i, :, 0:SHARE].astype(F32)

    squares = jnp.sum(resid * resid, axis=1, keepdims=True)
    high = squares.astype(BF16).astype(F32)
    low = squares - high
    beside = lax.broadcasted_iota(jnp.int32, (T, WIDE - SHARE), 1)
    tail = jnp.where(beside == 0, high, jnp.where(beside == 1, low, 0.0))
    gains = jnp.concatenate([gain_ref[pl.ds(x * 7 + i, 1), :] for i in range(7)], axis=1)
    gain = jnp.where(y == 0, gains[:, 0:SHARE], gains[:, SHARE:])
    scaled = jnp.concatenate([resid * gain, tail], axis=1).astype(BF16)
    row = lax.broadcasted_iota(jnp.int32, (GRID, T), 0)
    where = row.astype(F32)
    fourth = row % 4 == 3

    def chosen(at):
        return (at == place_rows[0]) | (at == place_rows[1])

    def pick(mask):
        return jnp.where(mask, 1.0, 0.0).astype(BF16)

    tails = [
        dot(pick(chosen(where - (3 - i)) & fourth), scaled[:, MAIN:WIDE]) for i in range(3)
    ]
    xs[...] = (
        dot(pick(chosen(where)), scaled[:, 0:MAIN]) + jnp.concatenate(tails, axis=1)
    ).astype(BF16)

    def rows16(i):
        return pl.ds(pl.multiple_of(i * 16, 16), 16)

    def exchange(src, dst, sems):
        def go(i, carry):
            to = (e + i) % NEXP
            here, there = src.at[rows16(to)], dst.at[rows16(e)]
            remote(here, there, sems.at[0], sems.at[1], exp=to).start()
            return carry

        lax.fori_loop(1, NEXP, go, 0)
        dst[rows16(e), :] = src[rows16(e), :]
        everything = pl.ds(0, (NEXP - 1) * 16)
        all_sent = remote(src.at[everything], dst.at[everything], sems.at[0], sems.at[1], exp=sibling)
        all_sent.wait_recv()
        return all_sent

    a_left = exchange(xs, rx, a_sems)
    for j in range(4):
        rows = slice(j * ROWS, (j + 1) * ROWS)
        xa[c, j, :, 0:MAIN] = dot(perm[0, rows, :], rx[...]).astype(BF16)
        tail = sum(dot(perm[1 + i, rows, :], rx[:, i * 128 : (i + 1) * 128]) for i in range(3))
        xa[c, j, :, MAIN:WIDE] = tail.astype(BF16)

    def rows_view(j):
        return lambda block, first, rows: xa.at[block, j, pl.ds(first, rows)]

    gathers = [Gather(rows_view(j), ROWS, g_send.at[0], g_recv.at[j], around) for j in range(4)]
    for g in gathers:
        g.first()

    lanes = lax.broadcasted_iota(jnp.int32, (ROWS, 128), 1)

    def expert(j):
        gathers[j].arrived(3)
        gathers[j].arrived(4)

        def feed(block, carry):
            g, u, t = carry
            rows_c = pl.ds(pl.multiple_of(block * SHARE, SHARE), SHARE)
            lhs = xa[block, j, :, 0:SHARE]
            g = g + dot(lhs, wg[j, rows_c, :])
            u = u + dot(lhs, wu[j, rows_c, :])
            return g, u, t + xa[block, j, :, 384:WIDE].astype(F32)

        zero = jnp.zeros((ROWS, FFL), F32)
        g, u, t = lax.fori_loop(0, NCTX, feed, (zero, zero, zero))
        kept = jnp.where((lanes == 64) | (lanes == 65), t, 0.0)
        inv = lax.rsqrt(jnp.sum(kept, axis=1, keepdims=True) / D + 1e-06)
        g, u = g * inv, u * inv
        act = (g / (1.0 + jnp.exp(-g)) * u).astype(BF16)

        def produce(xx, carry):
            cols = pl.ds(pl.multiple_of(xx * 2 * SHARE, 2 * SHARE), 2 * SHARE)
            both = dot(act, wd[j, :, cols]).astype(BF16)
            blank = jnp.zeros((ROWS, WIDE - SHARE), BF16)
            pd[xx * 2, j, :, 0:SHARE] = both[:, 0:SHARE]
            pd[xx * 2 + 1, j, :, 0:SHARE] = both[:, SHARE:]
            pd[xx * 2, j, :, SHARE:WIDE] = blank
            pd[xx * 2 + 1, j, :, SHARE:WIDE] = blank
            return carry

        lax.fori_loop(0, NCTX // 2, produce, 0)
        for i in (0, 1, 2, 6, 7):
            scopy(j, i).start()

    half = ROWS // 2
    lo, hi, whole = pl.ds(0, half), pl.ds(half, half), pl.ds(0, ROWS)
    yp, xr, xl = around.at(0, True), around.at(1, False), around.at(-1, False)
    sends = [
        (around.at(2, True), whole, 0, yp),
        (around.at(1, True), whole, 1, xr),
        (around.at(-1, True), whole, 2, xl),
        (around.at(2, False), lo, 3, xr),
        (around.at(2, False), hi, 4, xl),
        (around.at(0, True), whole, 5, yp),
        (around.at(1, False), hi, 6, xr),
        (around.at(-1, False), lo, 7, xl),
        (around.at(1, False), lo, 6, xr),
        (around.at(-1, False), hi, 7, xl),
    ]

    groups_of = (0, 1, 1, 2, 2, 3, 3, 3, 3, 3)
    whole_blocks = (1, 2, 1, 3)

    def scopy(j, i):
        block, rows, land, to = sends[i]
        here, there = pd.at[block, j, rows], tb.at[land, j, rows]
        return remote(here, there, s_send.at[0], s_recv.at[j, groups_of[i]], ctx=to)

    def sgot(j, group):
        here = tb.at[pl.ds(0, whole_blocks[group]), j]
        remote(here, here, s_send.at[0], s_recv.at[j, group], ctx=yp).wait_recv()

    def add(j, block, rows, *lands):
        total = pd[block, j, rows, :].astype(F32)
        for land in lands:
            total = total + tb[land, j, rows, :].astype(F32)
        pd[block, j, rows, :] = total.astype(BF16)

    def reduce1(j):
        sgot(j, 0)
        add(j, around.at(2, False), whole, 0)
        scopy(j, 3).start()
        scopy(j, 4).start()
        sgot(j, 1)
        add(j, around.at(0, True), whole, 1, 2)
        scopy(j, 5).start()

    def reduce2(j):
        sgot(j, 2)
        add(j, around.at(1, False), lo, 3)
        scopy(j, 8).start()
        add(j, around.at(-1, False), hi, 4)
        scopy(j, 9).start()

    def reduce3(j):
        sgot(j, 3)
        total = pd[c, j].astype(F32)
        for land in (5, 6, 7):
            total = total + tb[land, j].astype(F32)
        fin[j * ROWS : (j + 1) * ROWS, :] = total.astype(BF16)

    gathers[0].spread()
    gathers[0].halves()
    gathers[1].spread()
    gathers[1].halves()
    gathers[0].cross()
    gathers[2].spread()
    gathers[2].halves()
    gathers[3].spread()
    gathers[3].halves()
    gathers[1].cross()
    expert(0)
    gathers[2].cross()
    gathers[3].cross()
    expert(1)
    reduce1(0)
    expert(2)
    reduce1(1)
    reduce2(0)
    expert(3)
    reduce1(2)
    reduce2(1)
    reduce3(0)
    reduce1(3)
    reduce2(2)
    reduce3(1)
    reduce2(3)
    reduce3(2)
    reduce3(3)
    tails = [dot(unperm[1 + i], fin[:, MAIN:WIDE]) for i in range(3)]
    ys[...] = (dot(unperm[0], fin[:, 0:MAIN]) + jnp.concatenate(tails, axis=1)).astype(BF16)

    b_left = exchange(ys, back, b_sems)
    spot = lax.broadcasted_iota(jnp.int32, (T, GRID), 1)
    spots = spot.astype(F32)
    fourth = spot % 4 == 3
    result = resid
    for i in range(TOPK):
        main = dot(pick(spots == place_cols[i]), back[...])
        tail = sum(
            dot(
                pick((spots - (3 - n) == place_cols[i]) & fourth),
                back[:, n * 128 : (n + 1) * 128],
            )
            for n in range(3)
        )
        both = jnp.concatenate([main, tail[:, 0 : SHARE - MAIN]], axis=1)
        result = result + both * column(weight_ref[i : i + 1, :])
    out_ref[...] = result.astype(BF16)

    for p, group in ((0, 0), (3, 1), (5, 2)):
        wcopy(p, pieces(p, NEXP - 1), w_recv.at[0, 0], sibling).wait_send()
    seven = pl.ds(0, NCTX - 1)
    for sent, sem in (
        (latb.at[seven, pl.ds(0, MASKED)], l_send),
        (parts.at[seven], r_send),
        (xa.at[seven], g_send),
        (pd.at[seven], s_send),
    ):
        remote(sent, sent, sem.at[0], r_recv.at[0], ctx=yp).wait_send()
    a_left.wait_send()
    b_left.wait_send()


def permutations():
    perm = np.zeros((4, SLOTS, GRID), np.float32)
    for j in range(4):
        for s in range(NEXP):
            for i in range(3):
                perm[0, j * ROWS + s * 3 + i, s * 16 + j * 4 + i] = 1.0
                perm[1 + i, j * ROWS + s * 3 + i, s * 16 + j * 4 + 3] = 1.0
    return perm


VMEM = pl.BlockSpec(memory_space=pltpu.VMEM)
ANY = pl.BlockSpec(memory_space=pl.ANY)


def local(
    query,
    latent_cache,
    absorb_key,
    absorb_value,
    out_weight,
    hidden,
    norm_gain,
    block_mask,
    routes,
    route_weight,
    w_gate,
    w_up,
    w_down,
):
    perm = permutations()
    dma = pltpu.SemaphoreType.DMA
    return pl.pallas_call(
        functools.partial(layer_kernel, scale=1.0 / math.sqrt(DN + DR)),
        out_shape=jax.ShapeDtypeStruct((T, SHARE), BF16),
        in_specs=[ANY] * 15,
        out_specs=VMEM,
        scratch_shapes=[
            pltpu.VMEM((NEXP, HL, 16, DN), BF16),
            pltpu.VMEM((NEXP, HL, 16, DV), BF16),
            pltpu.VMEM((NEXP, WO, HL * DV), BF16),
            pltpu.VMEM((NCTX, DEPTH, CHUNK), BF16),
            pltpu.VMEM((HL * T, DEPTH), BF16),
            pltpu.VMEM((2, 2, HL * T // 4, CHUNK), F32),
            pltpu.VMEM((HL * T, DC), F32),
            pltpu.VMEM((HL * T, 128), F32),
            pltpu.VMEM((HL * T, 128), F32),
            pltpu.VMEM((T, HL * DV), BF16),
            pltpu.VMEM((NCTX, T, WIDE), BF16),
            pltpu.VMEM((NCTX, T, WIDE), BF16),
            pltpu.VMEM((T, HL * (DN + DR)), BF16),
            pltpu.VMEM((SHARE, T), BF16),
            pltpu.VMEM((D // 128, 128), F32),
            pltpu.VMEM((32, 32), jnp.int32),
            pltpu.VMEM((TOPK, T), jnp.int32),
            pltpu.VMEM((TOPK, T), F32),
            pltpu.VMEM((4, SLOTS, GRID), BF16),
            pltpu.VMEM((4, GRID, SLOTS), BF16),
            pltpu.VMEM((4, D, FFL), BF16),
            pltpu.VMEM((4, D, FFL), BF16),
            pltpu.VMEM((4, FFL, D), BF16),
            pltpu.VMEM((GRID, MAIN), BF16),
            pltpu.VMEM((GRID, MAIN), BF16),
            pltpu.VMEM((NCTX, 4, ROWS, WIDE), BF16),
            pltpu.VMEM((NCTX, 4, ROWS, WIDE), BF16),
            pltpu.VMEM((8, 4, ROWS, WIDE), BF16),
            pltpu.VMEM((SLOTS, WIDE), BF16),
            pltpu.VMEM((GRID, MAIN), BF16),
            pltpu.VMEM((GRID, MAIN), BF16),
            dma((15,)),
            dma((3,)),
            dma((5, 8)),
            dma((10,)),
            dma((1,)),
            dma((2, 5)),
            dma((1,)),
            dma((1,)),
            dma((2,)),
            dma((1,)),
            dma((4, 5)),
            dma((1,)),
            dma((4, 4)),
            dma((2,)),
        ],
        compiler_params=pltpu.CompilerParams(
            collective_id=0, has_side_effects=True, vmem_limit_bytes=56 * 1024 * 1024
        ),
        name="layer",
    )(
        query,
        latent_cache[0].T,
        absorb_key.transpose(0, 2, 1),
        absorb_value,
        out_weight.T,
        hidden.T,
        norm_gain.reshape(D // 128, 128),
        block_mask,
        routes.T,
        route_weight.T,
        jnp.asarray(perm, BF16),
        jnp.asarray(perm.transpose(0, 2, 1), BF16),
        w_gate,
        w_up,
        w_down,
    )


def solution(mesh):
    in_specs = (
        P("exp", "ctx"),
        P("exp", "ctx", None),
        P("ctx", None, "exp"),
        P("ctx", "exp", None),
        P("ctx", "exp"),
        P("exp", "ctx"),
        P(),
        P(),
        P("exp", None),
        P("exp", None),
        P("exp", None, "ctx"),
        P("exp", None, "ctx"),
        P("exp", "ctx", None),
    )
    out_specs = P("exp", "ctx")
    return jax.shard_map(local, mesh=mesh, in_specs=in_specs, out_specs=out_specs, check_vma=False)
```

```python
import functools
import math

import jax
import jax.numpy as jnp
import numpy as np
from jax import lax
from jax.experimental import pallas as pl
from jax.experimental.pallas import tpu as pltpu
from jax.sharding import PartitionSpec as P

D = 3584
HL = 8
DN = 128
DR = 64
DC = 512
DV = 128
TOPK = 2
BLK = 128
SHARE = 448
WIDE = 512
MAIN = 384
T = 128
NCTX = 8
NEXP = 32
CHUNK = 512
SLOTS = 384
GRID = 512
FFL = 128
MESH = pl.DeviceIdType.MESH
F32 = jnp.float32
BF16 = jnp.bfloat16
NT = (((1,), (1,)), ((), ()))
NN = (((1,), (0,)), ((), ()))
NEG = -1e38
WO = 112
ROWS = 96
MASKED = DC + DR
CAUSAL = MASKED + 16
DEPTH = CAUSAL + T
HALF_LAT = (DC + DR) // 2
PIECE_ROWS = {1: (0, 48), 2: (48, 32), 4: (80, 32), 5: (0, WO)}
LAST_PIECE = 4

PLAN = (
    ("first", 0), ("latents", 0), ("latents", 1), ("first", 1), ("prepare",), ("ring", 0, 1, 0),
    ("partner", 0), ("first", 2), ("ring", 0, 2, 0), ("ring", 0, 1, 1), ("first", 4), ("halves", 0),
    ("ring", 0, 3, 0), ("spread", 0), ("ring", 0, 2, 1), ("ring", 1, 1, 0), ("ring", 0, 3, 1),
    ("ring", 2, 1, 0), ("ring", 4, 1, 0), ("first", 3), ("ring", 1, 2, 0), ("halves", 1), ("spread", 1),
    ("far", 0), ("ring", 2, 2, 0), ("partner", 1), ("cross", 0), ("absorb",), ("ring", 3, 1, 0),
    ("attend", 0, 0), ("partner", 3), ("partner", 2), ("attend", 0, 1), ("partner", 4), ("attend", 0, 2),
    ("ring", 1, 1, 1), ("attend", 0, 3), ("ring", 3, 1, 1), ("attend", 1, 0), ("cross", 1), ("ring", 3, 2, 0),
    ("ring", 2, 1, 1), ("attend", 1, 1), ("ring", 4, 1, 1), ("attend", 1, 2), ("ring", 4, 2, 0),
    ("ring", 3, 2, 1), ("attend", 1, 3), ("ring", 3, 3, 0), ("ring", 1, 2, 1), ("attend", 2, 0),
    ("attend", 2, 1), ("ring", 2, 2, 1), ("ring", 4, 2, 1), ("attend", 2, 2), ("ring", 3, 3, 1),
    ("ring", 1, 3, 0), ("attend", 2, 3), ("attend", 3, 0), ("ring", 2, 3, 0), ("attend", 3, 1),
    ("ring", 4, 3, 0), ("far", 3), ("ring", 1, 3, 1), ("ring", 2, 3, 1), ("ring", 4, 3, 1), ("attend", 3, 2),
    ("attend", 3, 3), ("values",), ("far", 1), ("far", 2), ("project", 0), ("project", 1), ("far", 4),
    ("project", -1), ("project", 2), ("project", -2), ("project", 3), ("project", -3), ("project", 4),
)


def dot(a, b, dims=NN):
    return lax.dot_general(a, b, dims, preferred_element_type=F32)


def remote(src, dst, send, recv, **where):
    return pltpu.make_async_remote_copy(
        src_ref=src, dst_ref=dst, send_sem=send, recv_sem=recv, device_id=where, device_id_type=MESH
    )


def place():
    c, e = lax.axis_index("ctx"), lax.axis_index("exp")
    x, y = c // 2, c % 2
    return c, e, x, y


class Around:
    def __init__(self, x, y):
        self.x, self.y = x, y

    def at(self, dx, flip):
        yy = 1 - self.y if flip else self.y
        return ((self.x + dx + 4) % 4) * 2 + yy


class Gather:
    GROUP = (0, 1, 1, 3, 4, 2, 2, 4)
    BLOCKS = (1, 2, 1, 1, 2)

    def __init__(self, view, rows, send, recv, around):
        self.view, self.rows, self.send, self.recv, self.a = view, rows, send, recv, around
        self.to = {"y": around.at(0, True), "r": around.at(1, False), "l": around.at(-1, False)}

    def op(self, i):
        a, half = self.a, self.rows // 2
        table = [
            ((0, False), (0, True), "y", 0, self.rows),
            ((0, False), (-1, False), "r", 0, self.rows),
            ((0, False), (1, False), "l", 0, self.rows),
            ((0, True), (-1, True), "r", 0, self.rows),
            ((0, True), (1, True), "l", 0, self.rows),
            ((-1, False), (2, False), "r", 0, half),
            ((1, False), (2, False), "l", half, half),
            ((2, False), (2, True), "y", 0, self.rows),
        ]
        src, got, to, first, rows = table[i]
        return a.at(*src), a.at(*got), self.to[to], first, rows

    def start(self, i, src=None):
        block, _, to, first, rows = self.op(i)
        here = self.view(block, first, rows)
        group = self.GROUP[i]
        remote(here if src is None else src, here, self.send, self.recv.at[group], ctx=to).start()

    def arrived(self, group):
        blocks = self.BLOCKS[group]
        here = self.view(pl.ds(0, blocks), 0, self.rows)
        remote(here, here, self.send, self.recv.at[group], ctx=self.to["y"]).wait_recv()

    def first(self):
        for i in range(3):
            self.start(i)

    def spread(self):
        self.arrived(0)
        self.start(3)
        self.start(4)

    def halves(self):
        self.arrived(1)
        self.start(5)
        self.start(6)

    def cross(self):
        self.arrived(2)
        self.start(7)


def layer_kernel(
    q_ref,
    lat_ref,
    ak_ref,
    av_ref,
    wo_ref,
    hid_ref,
    gain_hbm,
    mask_hbm,
    routes_hbm,
    weight_hbm,
    perm_ref,
    unperm_ref,
    wg_hbm,
    wu_hbm,
    wd_hbm,
    out_ref,
    gak,
    gav,
    gwo,
    latb,
    qlat,
    sbuf,
    acc,
    mmax,
    lsum,
    attn,
    parts,
    got,
    qb,
    hidb,
    gain_ref,
    mask_ref,
    routes_ref,
    weight_ref,
    perm,
    unperm,
    wg,
    wu,
    wd,
    xs,
    rx,
    xa,
    pd,
    tb,
    fin,
    ys,
    back,
    own_sem,
    w_send,
    w_recv,
    sib_recv,
    l_send,
    l_recv,
    r_send,
    r_recv,
    a_sems,
    g_send,
    g_recv,
    s_send,
    s_recv,
    b_sems,
    *,
    scale,
):
    c, e, x, y = place()
    z, h, k = e // 4, (e // 2) % 2, e % 2
    around = Around(x, y)

    def eid(zz, hh, kk):
        return ((zz + 16) % 8) * 4 + hh * 2 + kk

    up, down = eid(z + 1, h, k), eid(z - 1, h, k)
    partner, sibling = eid(z, 1 - h, k), eid(z, h, 1 - k)

    local_copies = [
        pltpu.make_async_copy(src, dst, own_sem.at[i])
        for i, (src, dst) in enumerate(
            (
                (ak_ref, gak.at[e]),
                (lat_ref, latb.at[c, pl.ds(0, MASKED)]),
                (av_ref, gav.at[e]),
                (wo_ref, gwo.at[e]),
                (wg_hbm, wg),
                (wu_hbm, wu),
                (wd_hbm, wd),
                (q_ref, qb),
                (hid_ref, hidb),
                (perm_ref, perm),
                (unperm_ref, unperm),
                (mask_hbm, mask_ref),
                (gain_hbm, gain_ref),
                (routes_hbm, routes_ref),
                (weight_hbm, weight_ref),
            )
        )
    ]
    early = local_copies[:4] + [local_copies[7]]
    mask_copy = local_copies[11]
    late = local_copies[4:7] + local_copies[8:11] + local_copies[12:]

    barrier = pltpu.get_barrier_semaphore()

    peers = [{"exp": d} for d in (up, down, partner, sibling)]
    peers += [{"ctx": (c + i) % NCTX} for i in range(1, NCTX)]
    for where in peers:
        pl.semaphore_signal(barrier, inc=1, device_id=where, device_id_type=MESH)
    for copy in early + [mask_copy]:
        copy.start()
    pl.semaphore_wait(barrier, len(peers))


    def piece(p, block):
        if p == 0:
            return gak.at[block]
        if p == 3:
            return gav.at[block]
        return gwo.at[block, pl.ds(*PIECE_ROWS[p])]

    def own_piece(p):
        if p == 0:
            return ak_ref
        if p == 3:
            return av_ref
        return wo_ref.at[pl.ds(*PIECE_ROWS[p])]

    def slot(off, flip, other=False):
        return eid(z + off, 1 - h if flip else h, 1 - k if other else k)

    def group_of(p):
        return {0: 0, 3: 1}.get(p, 2)

    def wcopy(p, ref, sem, to, src=None):
        return remote(ref if src is None else src, ref, w_send.at[group_of(p)], sem, exp=to)

    def ring_sem(p, off, flip):
        return w_recv.at[p, 7 if off == 4 else 1 + (off - 1) * 2 + int(flip)]

    def sibling_sem(p, off):
        return sib_recv.at[off % 8 + 2] if p == 5 else sib_recv.at[group_of(p)]

    def send_on(p, off, flip, sign, own=False):
        here = piece(p, slot(-sign * off, flip))
        src = own_piece(p) if own else None
        wcopy(p, here, ring_sem(p, off + 1, flip), up if sign > 0 else down, src).start()

    def send_sibling(p, off, flip, own=False):
        if p == LAST_PIECE:
            p = 5
        if p in (0, 3, 5):
            here = piece(p, slot(off, flip))
            wcopy(p, here, sibling_sem(p, off), sibling, own_piece(p) if own else None).start()

    def pieces(p, count):
        if p == 0:
            return gak.at[pl.ds(0, count)]
        if p == 3:
            return gav.at[pl.ds(0, count)]
        return gwo.at[pl.ds(0, count), pl.ds(*PIECE_ROWS[p])]

    def weights_first(p):
        for sign in (1, -1):
            send_on(p, 0, False, sign, True)
        wcopy(p, piece(p, e), w_recv.at[p, 0], partner, own_piece(p)).start()
        send_sibling(p, 0, False, True)

    def weights_partner(p):
        wcopy(p, pieces(p, 1), w_recv.at[p, 0], partner).wait_recv()
        for sign in (1, -1):
            send_on(p, 0, True, sign)
        send_sibling(p, 0, True)

    def weights_ring(p, off, flip):
        wcopy(p, pieces(p, 2), ring_sem(p, off, flip), partner).wait_recv()
        for sign in (1, -1):
            if off < 3 or flip == (sign < 0):
                send_on(p, off, flip, sign)
            send_sibling(p, -sign * off, flip)

    def weights_far(p):
        wcopy(p, pieces(p, 2), ring_sem(p, 4, False), partner).wait_recv()
        for flip in (False, True):
            send_sibling(p, 4, flip)

    def weights_sibling(p, off, count):
        wcopy(p, pieces(p, count), sibling_sem(p, off), sibling).wait_recv()

    def latent_view(base):
        return lambda block, first, rows: latb.at[block, pl.ds(base + first, rows)]

    lats = [
        Gather(latent_view(i * HALF_LAT), HALF_LAT, l_send.at[0], l_recv.at[i], around)
        for i in range(2)
    ]

    def latents_first(i):
        for op in range(3):
            lats[i].start(op, lat_ref.at[pl.ds(i * HALF_LAT, HALF_LAT)])

    def prepare():
        for copy in late:
            copy.start()
        mask_copy.wait()
        blocks = NCTX * CHUNK // BLK
        last = mask_ref[blocks - 1 : blocks, :].astype(F32)
        at = lax.broadcasted_iota(jnp.int32, (1, blocks), 1)
        top = lax.broadcasted_iota(jnp.int32, (16, BLK), 0) == 0

        def fill(i, carry):
            for b in range(CHUNK // BLK):
                cols = slice(b * BLK, (b + 1) * BLK)
                here = at == i * (CHUNK // BLK) + b
                is_open = jnp.sum(jnp.where(here, last, 0.0), axis=1, keepdims=True)
                taken = jnp.where(top, NEG, 0.0) * (1.0 - is_open)
                latb[i, MASKED:CAUSAL, cols] = taken.astype(BF16)
            latb[i, CAUSAL:DEPTH, :] = jnp.zeros((T, CHUNK), BF16)
            return carry

        lax.fori_loop(0, NCTX, fill, 0)
        latb[NCTX - 1, CAUSAL:DEPTH, CHUNK - T : CHUNK] = jnp.where(lane > sub, NEG, 0.0).astype(BF16)
        ones = jnp.where(lane[:, 0:16] == 0, 1.0, 0.0).astype(BF16)
        for head in range(HL):
            qlat[head * T : (head + 1) * T, MASKED:CAUSAL] = ones
            qlat[head * T : (head + 1) * T, CAUSAL:DEPTH] = eye

    sub = lax.broadcasted_iota(jnp.int32, (T, T), 0)
    lane = lax.broadcasted_iota(jnp.int32, (T, T), 1)
    eye = jnp.where(sub == lane, 1.0, 0.0).astype(BF16)

    def column(row):
        return jnp.sum(jnp.where(sub == lane, row, 0.0), axis=1, keepdims=True)

    def places():
        earlier = jnp.where(sub < lane, 1.0, 0.0).astype(BF16)
        expert_of_row = sub.astype(F32)
        routes = [routes_ref[i : i + 1, :].astype(F32) for i in range(TOPK)]
        named = [jnp.where(expert_of_row == r, 1.0, 0.0) for r in routes]
        before = dot((named[0] + named[1]).astype(BF16), earlier)
        return [
            r * 4 + jnp.sum(before * n, axis=0, keepdims=True)
            for r, n in zip(routes, named, strict=True)
        ]

    def absorb():
        weights_sibling(0, 0, 16)
        for copy in early:
            copy.wait()

        def body(i, carry):
            pair_q = qb[:, pl.ds(pl.multiple_of(i * 384, 384), 384)]
            for j in range(2):
                at = j * (DN + DR)
                rows = pl.ds(pl.multiple_of(i * 2 * T + j * T, T), T)
                weight = gak[:, pl.ds(i * 2 + j, 1)].reshape(DC, DN)
                qlat[rows, 0:DC] = (dot(pair_q[:, at : at + DN], weight, NT) * factor).astype(BF16)
                rope = pair_q[:, at + DN : at + DN + DR].astype(F32) * factor
                qlat[rows, DC : DC + DR] = rope.astype(BF16)
            return carry

        lax.fori_loop(0, HL // 2, body, 0)

    factor = scale * math.log2(math.e)
    groups = [
        [around.at(0, False), around.at(0, True)],
        [around.at(-1, False), around.at(1, False)],
        [around.at(2, False), around.at(-1, True)],
        [around.at(1, True), around.at(2, True)],
    ]
    step_rows = HL * T // 4

    def score(g, q):
        rows = pl.ds(q * step_rows, step_rows)
        for i, b in enumerate(groups[g]):
            sbuf[q % 2, i] = dot(qlat[rows, :], latb[b])

    def attend(g, q):
        if q == 0:
            for piece_of in lats:
                if g == 2:
                    piece_of.arrived(3)
                if g == 3:
                    piece_of.arrived(4)
            score(g, 0)
        if q < 3:
            score(g, q + 1)
        rows = pl.ds(q * step_rows, step_rows)
        scores = [sbuf[q % 2, i] for i in range(2)]
        top = jnp.max(jnp.maximum(*scores), axis=1, keepdims=True)
        if g > 0:
            old = mmax[rows, 0:1]
            top = jnp.maximum(old, top)
        probs = [jnp.exp2(s - top) for s in scores]
        total = jnp.sum(probs[0] + probs[1], axis=1, keepdims=True)
        product = sum(
            dot(p.astype(BF16), latb[b, 0:DC, :], NT)
            for p, b in zip(probs, groups[g], strict=True)
        )
        if g > 0:
            shrink = jnp.exp2(old - top)
            total = total + lsum[rows, 0:1] * shrink
            product = product + acc[rows, :] * shrink
        mmax[rows, :] = jnp.broadcast_to(top, (step_rows, 128))
        lsum[rows, :] = jnp.broadcast_to(total, (step_rows, 128))
        acc[rows, :] = product

    def values():
        weights_sibling(3, 0, 16)

        def body(head, carry):
            cols = pl.ds(pl.multiple_of(head * DV, DV), DV)
            rows = pl.ds(pl.multiple_of(head * T, T), T)
            weight = gav[:, pl.ds(head, 1)].reshape(DC, DV)
            latent_out = (acc[rows, :] * (1.0 / lsum[rows, 0:1])).astype(BF16)
            attn[:, cols] = dot(latent_out, weight).astype(BF16)
            return carry

        lax.fori_loop(0, HL, body, 0)


    def rcopy(dest, source):
        return remote(parts.at[dest], got.at[source], r_send.at[0], r_recv.at[0], ctx=dest)

    def project(off):
        weights_sibling(5, off, 2)
        dest = (z + off + 8) % 8
        weight = gwo[pl.ds(dest * 4, 4)].reshape(SHARE, HL * DV)
        partial = dot(attn[...], weight, NT)
        parts[dest, :, 0:SHARE] = partial.astype(BF16)
        parts[dest, :, SHARE:WIDE] = jnp.zeros((T, WIDE - SHARE), BF16)

        @pl.when(dest != c)
        def _():
            rcopy(dest, c).start()

        @pl.when(dest == c)
        def _():
            got[c] = parts[dest]

    acts = {
        "first": weights_first,
        "partner": weights_partner,
        "ring": weights_ring,
        "far": weights_far,
        "latents": latents_first,
        "spread": lambda i: lats[i].spread(),
        "halves": lambda i: lats[i].halves(),
        "cross": lambda i: lats[i].cross(),
        "prepare": prepare,
        "absorb": absorb,
        "attend": attend,
        "values": values,
        "project": project,
    }
    for act, *how in PLAN:
        acts[act](*how)

    here = got.at[pl.ds(0, NCTX - 1)]
    remote(here, here, r_send.at[0], r_recv.at[0], ctx=around.at(0, True)).wait_recv()
    for copy in late:
        copy.wait()
    place_rows = places()
    place_cols = [column(r) for r in place_rows]
    resid = dot(eye, hidb[...], NT)
    for i in range(NCTX):
        resid = resid + got[i, :, 0:SHARE].astype(F32)

    squares = jnp.sum(resid * resid, axis=1, keepdims=True)
    high = squares.astype(BF16).astype(F32)
    low = squares - high
    beside = lax.broadcasted_iota(jnp.int32, (T, WIDE - SHARE), 1)
    tail = jnp.where(beside == 0, high, jnp.where(beside == 1, low, 0.0))
    gains = jnp.concatenate([gain_ref[pl.ds(x * 7 + i, 1), :] for i in range(7)], axis=1)
    gain = jnp.where(y == 0, gains[:, 0:SHARE], gains[:, SHARE:])
    scaled = jnp.concatenate([resid * gain, tail], axis=1).astype(BF16)
    row = lax.broadcasted_iota(jnp.int32, (GRID, T), 0)
    where = row.astype(F32)
    fourth = row % 4 == 3

    def chosen(at):
        return (at == place_rows[0]) | (at == place_rows[1])

    def pick(mask):
        return jnp.where(mask, 1.0, 0.0).astype(BF16)

    tails = [
        dot(pick(chosen(where - (3 - i)) & fourth), scaled[:, MAIN:WIDE]) for i in range(3)
    ]
    xs[...] = (
        dot(pick(chosen(where)), scaled[:, 0:MAIN]) + jnp.concatenate(tails, axis=1)
    ).astype(BF16)

    def rows16(i):
        return pl.ds(pl.multiple_of(i * 16, 16), 16)

    def exchange(src, dst, sems):
        def go(i, carry):
            to = (e + i) % NEXP
            here, there = src.at[rows16(to)], dst.at[rows16(e)]
            remote(here, there, sems.at[0], sems.at[1], exp=to).start()
            return carry

        lax.fori_loop(1, NEXP, go, 0)
        dst[rows16(e), :] = src[rows16(e), :]
        everything = pl.ds(0, (NEXP - 1) * 16)
        all_sent = remote(src.at[everything], dst.at[everything], sems.at[0], sems.at[1], exp=sibling)
        all_sent.wait_recv()
        return all_sent

    a_left = exchange(xs, rx, a_sems)
    for j in range(4):
        rows = slice(j * ROWS, (j + 1) * ROWS)
        xa[c, j, :, 0:MAIN] = dot(perm[0, rows, :], rx[...]).astype(BF16)
        tail = sum(dot(perm[1 + i, rows, :], rx[:, i * 128 : (i + 1) * 128]) for i in range(3))
        xa[c, j, :, MAIN:WIDE] = tail.astype(BF16)

    def rows_view(j):
        return lambda block, first, rows: xa.at[block, j, pl.ds(first, rows)]

    gathers = [Gather(rows_view(j), ROWS, g_send.at[0], g_recv.at[j], around) for j in range(4)]
    for g in gathers:
        g.first()

    lanes = lax.broadcasted_iota(jnp.int32, (ROWS, 128), 1)

    def expert(j):
        gathers[j].arrived(3)
        gathers[j].arrived(4)

        def feed(block, carry):
            g, u, t = carry
            rows_c = pl.ds(pl.multiple_of(block * SHARE, SHARE), SHARE)
            lhs = xa[block, j, :, 0:SHARE]
            g = g + dot(lhs, wg[j, rows_c, :])
            u = u + dot(lhs, wu[j, rows_c, :])
            return g, u, t + xa[block, j, :, 384:WIDE].astype(F32)

        zero = jnp.zeros((ROWS, FFL), F32)
        g, u, t = lax.fori_loop(0, NCTX, feed, (zero, zero, zero))
        kept = jnp.where((lanes == 64) | (lanes == 65), t, 0.0)
        inv = lax.rsqrt(jnp.sum(kept, axis=1, keepdims=True) / D + 1e-06)
        g, u = g * inv, u * inv
        act = (g / (1.0 + jnp.exp(-g)) * u).astype(BF16)

        def produce(xx, carry):
            cols = pl.ds(pl.multiple_of(xx * 2 * SHARE, 2 * SHARE), 2 * SHARE)
            both = dot(act, wd[j, :, cols]).astype(BF16)
            blank = jnp.zeros((ROWS, WIDE - SHARE), BF16)
            pd[xx * 2, j, :, 0:SHARE] = both[:, 0:SHARE]
            pd[xx * 2 + 1, j, :, 0:SHARE] = both[:, SHARE:]
            pd[xx * 2, j, :, SHARE:WIDE] = blank
            pd[xx * 2 + 1, j, :, SHARE:WIDE] = blank
            return carry

        lax.fori_loop(0, NCTX // 2, produce, 0)
        for i in (0, 1, 2, 6, 7):
            scopy(j, i).start()

    half = ROWS // 2
    lo, hi, whole = pl.ds(0, half), pl.ds(half, half), pl.ds(0, ROWS)
    yp, xr, xl = around.at(0, True), around.at(1, False), around.at(-1, False)
    sends = [
        (around.at(2, True), whole, 0, yp),
        (around.at(1, True), whole, 1, xr),
        (around.at(-1, True), whole, 2, xl),
        (around.at(2, False), lo, 3, xr),
        (around.at(2, False), hi, 4, xl),
        (around.at(0, True), whole, 5, yp),
        (around.at(1, False), hi, 6, xr),
        (around.at(-1, False), lo, 7, xl),
        (around.at(1, False), lo, 6, xr),
        (around.at(-1, False), hi, 7, xl),
    ]

    groups_of = (0, 1, 1, 2, 2, 3, 3, 3, 3, 3)
    whole_blocks = (1, 2, 1, 3)

    def scopy(j, i):
        block, rows, land, to = sends[i]
        here, there = pd.at[block, j, rows], tb.at[land, j, rows]
        return remote(here, there, s_send.at[0], s_recv.at[j, groups_of[i]], ctx=to)

    def sgot(j, group):
        here = tb.at[pl.ds(0, whole_blocks[group]), j]
        remote(here, here, s_send.at[0], s_recv.at[j, group], ctx=yp).wait_recv()

    def add(j, block, rows, *lands):
        total = pd[block, j, rows, :].astype(F32)
        for land in lands:
            total = total + tb[land, j, rows, :].astype(F32)
        pd[block, j, rows, :] = total.astype(BF16)

    def reduce1(j):
        sgot(j, 0)
        add(j, around.at(2, False), whole, 0)
        scopy(j, 3).start()
        scopy(j, 4).start()
        sgot(j, 1)
        add(j, around.at(0, True), whole, 1, 2)
        scopy(j, 5).start()

    def reduce2(j):
        sgot(j, 2)
        add(j, around.at(1, False), lo, 3)
        scopy(j, 8).start()
        add(j, around.at(-1, False), hi, 4)
        scopy(j, 9).start()

    def reduce3(j):
        sgot(j, 3)
        total = pd[c, j].astype(F32)
        for land in (5, 6, 7):
            total = total + tb[land, j].astype(F32)
        fin[j * ROWS : (j + 1) * ROWS, :] = total.astype(BF16)

    gathers[0].spread()
    gathers[0].halves()
    gathers[1].spread()
    gathers[1].halves()
    gathers[0].cross()
    gathers[2].spread()
    gathers[2].halves()
    gathers[3].spread()
    gathers[3].halves()
    gathers[1].cross()
    expert(0)
    gathers[2].cross()
    gathers[3].cross()
    expert(1)
    reduce1(0)
    expert(2)
    reduce1(1)
    reduce2(0)
    expert(3)
    reduce1(2)
    reduce2(1)
    reduce3(0)
    reduce1(3)
    reduce2(2)
    reduce3(1)
    reduce2(3)
    reduce3(2)
    reduce3(3)
    tails = [dot(unperm[1 + i], fin[:, MAIN:WIDE]) for i in range(3)]
    ys[...] = (dot(unperm[0], fin[:, 0:MAIN]) + jnp.concatenate(tails, axis=1)).astype(BF16)

    b_left = exchange(ys, back, b_sems)
    spot = lax.broadcasted_iota(jnp.int32, (T, GRID), 1)
    spots = spot.astype(F32)
    fourth = spot % 4 == 3
    result = resid
    for i in range(TOPK):
        main = dot(pick(spots == place_cols[i]), back[...])
        tail = sum(
            dot(
                pick((spots - (3 - n) == place_cols[i]) & fourth),
                back[:, n * 128 : (n + 1) * 128],
            )
            for n in range(3)
        )
        both = jnp.concatenate([main, tail[:, 0 : SHARE - MAIN]], axis=1)
        result = result + both * column(weight_ref[i : i + 1, :])
    out_ref[...] = result.astype(BF16)

    for p, group in ((0, 0), (3, 1), (5, 2)):
        wcopy(p, pieces(p, NEXP - 1), w_recv.at[0, 0], sibling).wait_send()
    seven = pl.ds(0, NCTX - 1)
    for sent, sem in (
        (latb.at[seven, pl.ds(0, MASKED)], l_send),
        (parts.at[seven], r_send),
        (xa.at[seven], g_send),
        (pd.at[seven], s_send),
    ):
        remote(sent, sent, sem.at[0], r_recv.at[0], ctx=yp).wait_send()
    a_left.wait_send()
    b_left.wait_send()


def permutations():
    perm = np.zeros((4, SLOTS, GRID), np.float32)
    for j in range(4):
        for s in range(NEXP):
            for i in range(3):
                perm[0, j * ROWS + s * 3 + i, s * 16 + j * 4 + i] = 1.0
                perm[1 + i, j * ROWS + s * 3 + i, s * 16 + j * 4 + 3] = 1.0
    return perm


VMEM = pl.BlockSpec(memory_space=pltpu.VMEM)
ANY = pl.BlockSpec(memory_space=pl.ANY)


def local(
    query,
    latent_cache,
    absorb_key,
    absorb_value,
    out_weight,
    hidden,
    norm_gain,
    block_mask,
    routes,
    route_weight,
    w_gate,
    w_up,
    w_down,
):
    perm = permutations()
    dma = pltpu.SemaphoreType.DMA
    return pl.pallas_call(
        functools.partial(layer_kernel, scale=1.0 / math.sqrt(DN + DR)),
        out_shape=jax.ShapeDtypeStruct((T, SHARE), BF16),
        in_specs=[ANY] * 15,
        out_specs=VMEM,
        scratch_shapes=[
            pltpu.VMEM((NEXP, HL, 16, DN), BF16),
            pltpu.VMEM((NEXP, HL, 16, DV), BF16),
            pltpu.VMEM((NEXP, WO, HL * DV), BF16),
            pltpu.VMEM((NCTX, DEPTH, CHUNK), BF16),
            pltpu.VMEM((HL * T, DEPTH), BF16),
            pltpu.VMEM((2, 2, HL * T // 4, CHUNK), F32),
            pltpu.VMEM((HL * T, DC), F32),
            pltpu.VMEM((HL * T, 128), F32),
            pltpu.VMEM((HL * T, 128), F32),
            pltpu.VMEM((T, HL * DV), BF16),
            pltpu.VMEM((NCTX, T, WIDE), BF16),
            pltpu.VMEM((NCTX, T, WIDE), BF16),
            pltpu.VMEM((T, HL * (DN + DR)), BF16),
            pltpu.VMEM((SHARE, T), BF16),
            pltpu.VMEM((D // 128, 128), F32),
            pltpu.VMEM((32, 32), jnp.int32),
            pltpu.VMEM((TOPK, T), jnp.int32),
            pltpu.VMEM((TOPK, T), F32),
            pltpu.VMEM((4, SLOTS, GRID), BF16),
            pltpu.VMEM((4, GRID, SLOTS), BF16),
            pltpu.VMEM((4, D, FFL), BF16),
            pltpu.VMEM((4, D, FFL), BF16),
            pltpu.VMEM((4, FFL, D), BF16),
            pltpu.VMEM((GRID, MAIN), BF16),
            pltpu.VMEM((GRID, MAIN), BF16),
            pltpu.VMEM((NCTX, 4, ROWS, WIDE), BF16),
            pltpu.VMEM((NCTX, 4, ROWS, WIDE), BF16),
            pltpu.VMEM((8, 4, ROWS, WIDE), BF16),
            pltpu.VMEM((SLOTS, WIDE), BF16),
            pltpu.VMEM((GRID, MAIN), BF16),
            pltpu.VMEM((GRID, MAIN), BF16),
            dma((15,)),
            dma((3,)),
            dma((5, 8)),
            dma((10,)),
            dma((1,)),
            dma((2, 5)),
            dma((1,)),
            dma((1,)),
            dma((2,)),
            dma((1,)),
            dma((4, 5)),
            dma((1,)),
            dma((4, 4)),
            dma((2,)),
        ],
        compiler_params=pltpu.CompilerParams(
            collective_id=0, has_side_effects=True, vmem_limit_bytes=56 * 1024 * 1024
        ),
        name="layer",
    )(
        query,
        latent_cache[0].T,
        absorb_key.transpose(0, 2, 1),
        absorb_value,
        out_weight.T,
        hidden.T,
        norm_gain.reshape(D // 128, 128),
        block_mask,
        routes.T,
        route_weight.T,
        jnp.asarray(perm, BF16),
        jnp.asarray(perm.transpose(0, 2, 1), BF16),
        w_gate,
        w_up,
        w_down,
    )


def solution(mesh):
    in_specs = (
        P("exp", "ctx"),
        P("exp", "ctx", None),
        P("ctx", None, "exp"),
        P("ctx", "exp", None),
        P("ctx", "exp"),
        P("exp", "ctx"),
        P(),
        P(),
        P("exp", None),
        P("exp", None),
        P("exp", None, "ctx"),
        P("exp", None, "ctx"),
        P("exp", "ctx", None),
    )
    out_specs = P("exp", "ctx")
    return jax.shard_map(local, mesh=mesh, in_specs=in_specs, out_specs=out_specs, check_vma=False)
```
